768 devices in a mesh: grp: 16 (over x, y_lo), shard: 48 (over z, y_hi, core).
Axes of the slice: x: 4, y: 8 (y_hi: 2, y_lo: 4; y = y_hi * 4 + y_lo), z: 12, core: 2. Of those that a mesh axis runs over, the one named last changes fastest.
Arguments:
- hidden: bfloat16 [6144, 4096], P(('grp', 'shard')), may hold values from -160 to 160
- norm_gain: float32 [4096], replicated, may hold values from 0.5 to 1.5
- gate_codes: bfloat16 [4096, 7296], P('grp', 'shard'), may hold values from -6 to 6
- gate_scales: float32 [32, 7296], P('grp', 'shard'), may hold values from 0.005 to 0.05
- up_codes: bfloat16 [4096, 7296], P('grp', 'shard'), may hold values from -6 to 6
- up_scales: float32 [32, 7296], P('grp', 'shard'), may hold values from 0.005 to 0.05
- down_codes: bfloat16 [4096, 7296], P('grp', 'shard'), may hold values from -6 to 6
- down_scales: float32 [32, 7296], P('grp', 'shard'), may hold values from 0.0058536613 to 0.05853661
- head: bfloat16 [4096, 100], replicated, may hold values from -1 to 1
- teacher: float32 [6144, 100], P('grp'), may hold values from -400 to 400
- targets: int32 [6144], P('grp'), may hold values from 0 to 99
Outputs:
- loss: float32 [6144], P(('grp', 'shard'))
- grad_gate: float32 [4096, 7296], P('grp', 'shard')
- grad_up: float32 [4096, 7296], P('grp', 'shard')
- grad_down: float32 [4096, 7296], P('grp', 'shard')
The draws below stay inside these ranges and needn't reach their ends.
All inputs are finite; a program needn't handle non-finite values.
Results may differ from the reference program's by a relative error of at most 0.023.
Values may be sent and summed in bfloat16 or wider, within the bound.
A program may use at most 32 MiB of HBM per device.

```python
import math
import jax
import jax.numpy as jnp
from jax import lax

D = 4096
FF = 7296
BINS = 100
BLOCK = 128
TOKENS = 6144
N_GRP = 16


def head_matrix(key):
    return jnp.clip(jax.random.normal(key, (D, BINS), jnp.float32), -6.0, 6.0) / math.sqrt(D)


def draw_head(key, part):
    return head_matrix(key).astype(jnp.bfloat16)


def draw_hidden(key, part):
    key = jax.random.fold_in(key, 7)
    keys = jax.random.split(key, 1)
    base = jnp.clip(jax.random.normal(keys[0], (TOKENS, D), jnp.float32), -6.0, 6.0)
    return jnp.clip(base, -160.0, 160.0).astype(jnp.bfloat16)


def draw_teacher(key, part):
    key = jax.random.fold_in(key, 11)
    keys = jax.random.split(key, 1)
    base = 3.0 * jnp.clip(jax.random.normal(keys[0], (TOKENS, BINS), jnp.float32), -6.0, 6.0)
    return base


def with_ends(drawn, rng, low, largest):
    longest = drawn.shape.index(max(drawn.shape))
    spots = []
    for shift in (0, 1):
        where = [jax.random.randint(jax.random.fold_in(rng, axis), (), 0, length) for axis, length in enumerate(drawn.shape)]
        where[longest] = (where[longest] + shift) % drawn.shape[longest]
        spots.append(tuple(where))
    return drawn.at[spots[0]].set(low).at[spots[1]].set(largest)


def level_of(key, extent, shards, smallest, high):
    loudness, own = 1.0, jax.random.fold_in(key, 6)
    for axis_at, shards_of in shards:
        heights = jnp.exp(jax.random.uniform(jax.random.fold_in(own, axis_at), (shards_of,), jnp.float32, smallest / len(shards), high / len(shards)))
        loudness = loudness * jnp.repeat(heights, extent[axis_at] // shards_of).reshape([-1 if axis == axis_at else 1 for axis in range(len(extent))])
    return loudness


def normal_values(key, shape, scale, most, pieces=(), kind=jnp.bfloat16):
    entries = jax.random.normal(key, shape, jnp.float32) * scale
    if len(pieces) > 0:
        entries = level_of(key, shape, pieces, -0.22, 0.18) * entries
    return jnp.clip(entries, min=-most, max=most).astype(kind)


def setup_inputs(seed: int = 0) -> dict:
    splits = jax.random.split(jax.random.key(seed), 12)
    return {
        "hidden": draw_hidden(jax.random.fold_in(splits[11], 71), 0),
        "norm_gain": jnp.clip(1.0 + 0.1 * jax.random.normal(splits[1], (D,), jnp.float32), 0.5, 1.5),
        "gate_codes": normal_values(splits[2], (D, FF), 1.0, 6.0, ((0, 16), (1, 48))),
        "gate_scales": jnp.clip(jnp.exp(math.log(0.05) - 2.3025851 * jax.random.uniform(splits[3], (D // BLOCK, FF), jnp.float32) ** level_of(splits[3], (D // BLOCK, FF), ((0, 16), (1, 48)), -0.2, 0.2)), 0.005, 0.05),
        "up_codes": normal_values(splits[4], (D, FF), 1.0, 6.0, ((0, 16), (1, 48))),
        "up_scales": jnp.clip(jnp.exp(math.log(0.05) - 2.3025851 * jax.random.uniform(splits[5], (D // BLOCK, FF), jnp.float32) ** level_of(splits[5], (D // BLOCK, FF), ((0, 16), (1, 48)), -0.2, 0.2)), 0.005, 0.05),
        "down_codes": normal_values(splits[6], (D, FF), 1.0, 6.0, ((0, 16), (1, 48))),
        "down_scales": jnp.clip(jnp.exp(math.log(0.05853661) - 2.3025851 * jax.random.uniform(splits[7], (D // BLOCK, FF), jnp.float32) ** level_of(splits[7], (D // BLOCK, FF), ((0, 16), (1, 48)), -0.2, 0.2)), 0.0058536613, 0.05853661),
        "head": draw_head(jax.random.fold_in(splits[11], 71), 0),
        "teacher": draw_teacher(jax.random.fold_in(splits[11], 71), 0),
        "targets": with_ends(jax.random.randint(splits[10], (TOKENS,), 0, BINS), jax.random.fold_in(splits[10], 1), 0, BINS - 1).astype(jnp.int32),
    }


eps = 1e-05
loss_scale = 64.0

def dequantize(codes, scales):
    rows, cols = codes.shape
    blocks = scales.shape[0]
    scaled = codes.astype(jnp.float32).reshape(blocks, rows // blocks, cols) * scales[:, None, :]
    return scaled.reshape(rows, cols).astype(jnp.bfloat16)

def log_softmax_rows(values):
    top = lax.optimization_barrier(jnp.max(values, axis=1, keepdims=True))
    shifted = values - top
    return shifted - jnp.log(lax.optimization_barrier(jnp.sum(jnp.exp(shifted), axis=1, keepdims=True)))

def reference(hidden, norm_gain, gate_codes, gate_scales, up_codes, up_scales, down_codes, down_scales, head, teacher, targets):
    x_float = hidden.astype(jnp.float32)
    normed = (x_float * lax.rsqrt(lax.optimization_barrier(jnp.mean(x_float * x_float, axis=1, keepdims=True)) + eps) * norm_gain).astype(jnp.bfloat16)
    w_gate = dequantize(gate_codes, gate_scales)
    w_up = dequantize(up_codes, up_scales)
    w_down = dequantize(down_codes, down_scales)
    gate = jnp.dot(normed, w_gate, preferred_element_type=jnp.float32)
    up = jnp.dot(normed, w_up, preferred_element_type=jnp.float32)
    sig = jax.nn.sigmoid(gate)
    act = gate * sig
    units = (act * up).astype(jnp.bfloat16)
    branch = jnp.dot(units, w_down.T, preferred_element_type=jnp.float32)
    head_float = head.astype(jnp.float32)
    logits = jnp.dot(x_float + branch, head_float, precision=lax.Precision.HIGHEST)
    log_student = log_softmax_rows(logits)
    log_teacher = log_softmax_rows(teacher)
    p_student = jnp.exp(log_student)
    p_teacher = jnp.exp(log_teacher)
    onehot = (jnp.arange(BINS, dtype=jnp.int32)[None, :] == targets[:, None]).astype(jnp.float32)
    loss = -lax.optimization_barrier(jnp.sum(onehot * log_student, axis=1)) + lax.optimization_barrier(jnp.sum(p_teacher * (log_teacher - log_student), axis=1))
    d_logits = loss_scale * (2.0 * p_student - onehot - p_teacher)
    d_branch = jnp.dot(d_logits, head_float.T, precision=lax.Precision.HIGHEST).astype(jnp.bfloat16)
    d_units = jnp.dot(d_branch, w_down, preferred_element_type=jnp.float32)
    d_gate = (d_units * up * sig * (1.0 + gate * (1.0 - sig))).astype(jnp.bfloat16)
    d_up = (d_units * act).astype(jnp.bfloat16)
    group_rows = TOKENS // N_GRP

    def rounded(left, right):
        partial_value = jnp.dot(left.T, right, preferred_element_type=jnp.float32).astype(jnp.bfloat16)
        return lax.optimization_barrier(partial_value).astype(jnp.float32)

    def add_group(carry, index):
        start = (index * group_rows).astype(jnp.int32)
        xs = lax.dynamic_slice_in_dim(normed, start, group_rows, 0)
        dg = lax.dynamic_slice_in_dim(d_gate, start, group_rows, 0)
        du = lax.dynamic_slice_in_dim(d_up, start, group_rows, 0)
        db = lax.dynamic_slice_in_dim(d_branch, start, group_rows, 0)
        hs = lax.dynamic_slice_in_dim(units, start, group_rows, 0)
        return ((carry[0] + rounded(xs, dg), carry[1] + rounded(xs, du), carry[2] + rounded(db, hs)), None)
    zeros = jnp.zeros((D, FF), jnp.float32)
    grads, unused = lax.scan(add_group, (zeros, zeros, zeros), jnp.arange(N_GRP, dtype=jnp.int32))
    return (loss, grads[0], grads[1], grads[2])
```

```python
import functools

import jax
import jax.numpy as jnp
from jax import lax
from jax.experimental import pallas as pl
from jax.experimental.pallas import tpu as pltpu
from jax.sharding import PartitionSpec as P

eps = 1e-05
loss_scale = 64.0
MESH = pl.DeviceIdType.MESH
f32, bf16 = jnp.float32, jnp.bfloat16

X, Y = 4, 4
H, C = 2, 2
CUT = 160
LANES = 128


def nt(left, right):
    return lax.dot_general(left, right, (((1,), (1,)), ((), ())), preferred_element_type=f32)


def nn(left, right):
    return jnp.dot(left, right, preferred_element_type=f32)


def tn(left, right):
    return lax.dot_general(left, right, (((0,), (0,)), ((), ())), preferred_element_type=f32)


def split(value):
    high = value.astype(bf16)
    return high, (value - high.astype(f32)).astype(bf16)


class Wires:
    def __init__(self, send_sems, recv_sems, names):
        self.send_sems, self.recv_sems, self.names, self.started = send_sems, recv_sems, names, []

    def slot(self, name):
        return self.names[name]

    def describe(self, name, src, dst, device):
        at = self.slot(name)
        return pltpu.make_async_remote_copy(
            src_ref=src,
            dst_ref=dst,
            send_sem=self.send_sems.at[at],
            recv_sem=self.recv_sems.at[at],
            device_id=device,
            device_id_type=MESH,
        )

    def send(self, name, src, dst, device):
        copy = self.describe(name, src, dst, device)
        copy.start()
        self.started.append(copy)

    def recv(self, name, dst, device):
        self.describe(name, dst, dst, device).wait_recv()

    def finish(self):
        for copy in self.started:
            copy.wait_send()


def wire_names(Z):
    half = Z // 2
    names = ["e", "hx", "l1", "l3", "l5"]
    for j in range(Y):
        names += [f"{kind}{j}" for kind in ("y", "xp", "xm", "fp", "fm", "ra", "rb", "sp", "sm", "ry")]
    for s in range(2):
        for n in range(1, half + 1):
            names += [f"zp{s}_{n}", f"zm{s}_{n}"]
        for k in range(-half, half + 1):
            names.append(f"c{s}_{k}")
    for k in range(1, Z):
        names += [f"l2_{k}", f"l4_{k}"]
    for kind in ("m", "n"):
        for k in range(1, X):
            names += [f"{kind}r{k}", f"{kind}a{k}"]
        for j in range(1, Y):
            names.append(f"{kind}y{j}")
    return {name: at for at, name in enumerate(names)}


def kernel(
    names, Z, D, F, B,
    hid, gain, gc, gs, uc, us, dc, ds, head, teach, targ,
    loss_o, gg_o, gu_o, gd_o,
    halves, pair, nb, wt, scale_pad, head_own, own_logit, teach_pad, teach_rows,
    acc, units_s, whole, mred, mrx, mry, nred, nrx, nry,
    part, l1_in, summed, l2_in, l3_out, l3_in, dl, loss_s,
    grads, ra, rb, sp, sm, ry,
    send_sems, recv_sems,
):
    grp, sh = lax.axis_index("grp"), lax.axis_index("shard")
    x, y = lax.div(grp, Y), lax.rem(grp, Y)
    z, h, c = lax.div(sh, H * C), lax.rem(lax.div(sh, C), H), lax.rem(sh, C)
    half = Z // 2
    RB = D // (X * Y)
    T8 = hid.shape[0]
    KH = D // 2

    def xat(dx):
        return lax.rem(x + dx % X, X) if dx % X else x

    def yat(j):
        return (y, y + 1 - 2 * lax.rem(y, 2), y + 2 - 4 * lax.div(y, 2), 3 - y)[j]

    def zat(dz):
        return lax.rem(z + dz % Z, Z) if dz % Z else z

    def to_x(dx):
        return {"grp": xat(dx) * Y + y}

    def to_y(j):
        return {"grp": x * Y + yat(j)}

    def to_z(dz):
        return {"shard": (zat(dz) * H + h) * C + c}

    to_h = {"shard": (z * H + (1 - h)) * C + c}
    to_c = {"shard": (z * H + h) * C + (1 - c)}

    wires = Wires(send_sems, recv_sems, names)
    send, recv = wires.send, wires.recv

    barrier = pltpu.get_barrier_semaphore()
    peers = [to_c, to_h] + [to_x(k) for k in range(1, X)] + [to_y(j) for j in range(1, Y)]
    peers += [to_z(k) for k in range(1, Z)]
    for peer in peers:
        pl.semaphore_signal(barrier, inc=1, device_id=peer, device_id_type=MESH)

    xf = hid[...].astype(f32)
    mean = jnp.mean(xf * xf, axis=1, keepdims=True)
    normed = (xf * lax.rsqrt(mean + eps) * gain[...]).astype(bf16).astype(f32)
    halves[0] = normed[:, :KH]
    halves[1] = normed[:, KH:]
    pair[c] = halves[c]

    scale_pad[...] = jnp.zeros_like(scale_pad)
    scale_pad[0:2, 0:F] = gs[...]
    scale_pad[8:10, 0:F] = us[...]
    scale_pad[16:18, 0:F] = ds[...]
    columns = scale_pad[...].T

    def dequantize(codes, at):
        value = codes[...].astype(f32)
        mid = RB // 2
        left = value[:, :mid] * columns[:F, at : at + 1]
        right = value[:, mid:] * columns[:F, at + 1 : at + 2]
        return jnp.concatenate([left, right], axis=1)

    wt[grp] = jnp.concatenate([dequantize(gc, 0), dequantize(uc, 8)], axis=0).astype(bf16)

    pl.semaphore_wait(barrier, len(peers))

    send("e", halves.at[1 - c], pair.at[c], to_c)
    send("xp0", wt.at[grp], wt.at[grp], to_x(1))
    send("xm0", wt.at[grp], wt.at[grp], to_x(-1))
    for j in range(1, Y):
        send(f"y{j}", wt.at[grp], wt.at[grp], to_y(j))

    def gat(dx, j):
        return xat(dx) * Y + yat(j)

    def spread_y(j):
        block = wt.at[gat(0, j)]
        recv(f"y{j}", block, to_y(j))
        send(f"xp{j}", block, block, to_x(1))
        send(f"xm{j}", block, block, to_x(-1))

    def forward_x(j):
        low, high = wt.at[gat(-1, j)], wt.at[gat(1, j)]
        recv(f"xp{j}", low, to_x(-1))
        send(f"fp{j}", low.at[pl.ds(0, CUT)], low.at[pl.ds(0, CUT)], to_x(1))
        recv(f"xm{j}", high, to_x(1))
        send(f"fm{j}", high.at[pl.ds(CUT, 2 * F - CUT)], high.at[pl.ds(CUT, 2 * F - CUT)], to_x(-1))

    def finish_x(j):
        far = wt.at[gat(2, j)]
        recv(f"fp{j}", far.at[pl.ds(0, CUT)], to_x(-1))
        recv(f"fm{j}", far.at[pl.ds(CUT, 2 * F - CUT)], to_x(1))

    def block_of(s, dz):
        return nb.at[c, zat(dz) * H + (h if s == 0 else 1 - h)]

    def other_block_of(s, dz):
        return nb.at[1 - c, zat(dz) * H + (h if s == 0 else 1 - h)]

    def start_z(s):
        block = block_of(s, 0)
        send(f"zp{s}_1", block, block, to_z(1))
        send(f"zm{s}_1", block, block, to_z(-1))
        send(f"c{s}_0", block, block, to_c)

    def column_half(ref, at):
        return ref.at[:, pl.ds(at * (KH // 2), KH // 2)]

    def step_z(s, n):
        low, high = block_of(s, -n), block_of(s, n)
        if n < half:
            recv(f"zp{s}_{n}", low, to_z(-1))
            if n + 1 < half:
                send(f"zp{s}_{n + 1}", low, low, to_z(1))
            else:
                send(f"zp{s}_{n + 1}", column_half(low, 0), column_half(low, 0), to_z(1))
            recv(f"zm{s}_{n}", high, to_z(1))
            if n + 1 < half:
                send(f"zm{s}_{n + 1}", high, high, to_z(-1))
            else:
                send(f"zm{s}_{n + 1}", column_half(high, 1), column_half(high, 1), to_z(-1))
            send(f"c{s}_{-n}", low, low, to_c)
            send(f"c{s}_{n}", high, high, to_c)
        else:
            recv(f"zp{s}_{n}", column_half(low, 0), to_z(-1))
            recv(f"zm{s}_{n}", column_half(low, 1), to_z(1))
            send(f"c{s}_{n}", low, low, to_c)

    def sum_start(kind, red, rx):
        for k in range(1, X):
            send(f"{kind}r{k}", red.at[xat(k)], rx.at[k - 1], to_x(k))

    def sum_middle(kind, red, rx, ry_):
        for k in range(1, X):
            recv(f"{kind}r{k}", rx.at[k - 1], to_x(-k))
        ry_[0] = red[x] + rx[0] + rx[1] + rx[2]
        for j in range(1, Y):
            send(f"{kind}y{j}", ry_.at[0], ry_.at[j], to_y(j))

    def sum_spread(kind, red, rx, ry_):
        for j in range(1, Y):
            recv(f"{kind}y{j}", ry_.at[j], to_y(j))
        rx[X - 1] = ry_[0] + ry_[1] + ry_[2] + ry_[3]
        for k in range(1, X):
            send(f"{kind}a{k}", rx.at[X - 1], ry_.at[Y + k - 1], to_x(k))

    def sum_end(kind, red, rx, ry_):
        whole[x] = rx[X - 1]
        for k in range(1, X):
            recv(f"{kind}a{k}", ry_.at[Y + k - 1], to_x(-k))
            whole[xat(-k)] = ry_[Y + k - 1]
        return whole[...].reshape(red.shape[0] * red.shape[1], LANES)[:F]

    recv("e", pair.at[1 - c], to_c)
    nb[c, z * H + h] = pair[...].reshape(2 * T8, KH).astype(bf16)
    own = block_of(0, 0)
    start_z(0)
    send("hx", own, own, to_h)

    head_own[...] = jnp.zeros_like(head_own)
    head_own[0:B, :] = head[:, pl.ds(pl.multiple_of(grp * RB, RB), RB)].astype(f32)
    head_block = head_own[...].astype(bf16)
    w_down = dequantize(dc, 16).astype(bf16)
    product = nt(w_down, head_block)
    rows = mred.shape[0] * mred.shape[1]
    tail = jnp.zeros((rows - F, LANES), f32)
    mred[...] = jnp.concatenate([product, tail], axis=0).reshape(mred.shape)
    sum_start("m", mred, mrx)

    own_logit[...] = jnp.zeros_like(own_logit)
    own_logit[:, 0:B] = nt(hid[...], head[...])
    teach_pad[...] = jnp.zeros_like(teach_pad)
    teach_pad[0:B, :] = teach[...]
    teach_rows[...] = teach_pad[...].T.reshape(teach_rows.shape)

    step_z(0, 1)
    forward_x(0)
    spread_y(1)
    recv("hx", block_of(1, 0), to_h)
    start_z(1)
    step_z(0, 2)
    sum_middle("m", mred, mrx, mry)
    step_z(1, 1)
    forward_x(1)
    spread_y(2)
    step_z(0, 3)
    step_z(1, 2)
    sum_spread("m", mred, mrx, mry)
    finish_x(0)
    forward_x(2)
    spread_y(3)
    for n in range(4, half + 1):
        step_z(0, n)
        step_z(1, n - 1)
        if n == 5:
            forward_x(3)
    step_z(1, half)
    big_m = sum_end("m", mred, mrx, mry)
    for j in range(1, Y):
        finish_x(j)
    for s in range(2):
        for k in range(-half + 1, half + 1):
            recv(f"c{s}_{k}", other_block_of(s, k), to_c)

    tokens = acc.shape[1]
    per = X * Y // 2

    def normed_columns(g):
        at = lax.rem(g, per)
        return nb[lax.div(g, per), :, :, pl.ds(pl.multiple_of(at * RB, RB), RB)].reshape(tokens, RB)

    acc[...] = jnp.zeros_like(acc)

    def add_block(g, carry):
        acc[...] += nt(wt[g], normed_columns(g))
        return carry

    lax.fori_loop(0, X * Y, add_block, 0)
    gate, up = acc[0:F, :], acc[F : 2 * F, :]
    sig = jax.nn.sigmoid(gate)
    units = (gate * sig * up).astype(bf16)
    units_s[...] = units.astype(f32)

    m_high, m_low = split(big_m)
    share = (tn(units, m_high) + tn(units, m_low)).reshape(Z * H, C, T8, LANES)
    part[0] = share[:, 0].reshape(Z, H, T8, LANES)
    part[1] = share[:, 1].reshape(Z, H, T8, LANES)
    send("l1", part.at[1 - c], l1_in, to_c)
    recv("l1", l1_in, to_c)
    summed[...] = part[c] + l1_in[...]
    for k in range(1, Z):
        send(f"l2_{k}", summed.at[zat(k)], l2_in.at[k - 1], to_z(k))
    total = summed[z]
    for k in range(1, Z):
        recv(f"l2_{k}", l2_in.at[k - 1], to_z(-k))
        total = total + l2_in[k - 1]
    l3_out[...] = total
    l3_out[h] = l3_out[h] + own_logit[...]
    send("l3", l3_out, l3_in, to_h)
    recv("l3", l3_in, to_h)
    logits = (l3_out[...] + l3_in[...]).reshape(H * T8, LANES)

    lane = lax.broadcasted_iota(jnp.int32, (H * T8, LANES), 1)
    sub = lax.broadcasted_iota(jnp.int32, (H * T8, LANES), 0)
    valid = lane < B
    first = (z * H * C + c) * T8
    wanted = jnp.zeros((H * T8, LANES), jnp.int32)
    for at in range(H * T8):
        value = targ[first + (at // T8) * C * T8 + at % T8]
        wanted = jnp.where(sub == at, value, wanted)
    onehot = jnp.where(lane == wanted, 1.0, 0.0)

    def log_softmax(values):
        top = jnp.max(jnp.where(valid, values, -jnp.inf), axis=1, keepdims=True)
        shifted = jnp.where(valid, values - top, 0.0)
        bottom = jnp.sum(jnp.where(valid, jnp.exp(shifted), 0.0), axis=1, keepdims=True)
        return shifted - jnp.log(bottom)

    teacher = jnp.concatenate([teach_rows[z * H * C + k * C + c] for k in range(H)], axis=0)
    log_student, log_teacher = log_softmax(logits), log_softmax(teacher)
    p_student, p_teacher = jnp.exp(log_student), jnp.exp(log_teacher)
    terms = jnp.where(valid, p_teacher * (log_teacher - log_student) - onehot * log_student, 0.0)
    loss = jnp.sum(terms, axis=1, keepdims=True)
    d_own = jnp.where(valid, loss_scale * (2.0 * p_student - onehot - p_teacher), 0.0)
    dl[c, z] = d_own.reshape(H, T8, LANES)
    for k in range(1, Z):
        send(f"l4_{k}", dl.at[c, z], dl.at[c, z], to_z(k))
    loss_s[...] = jnp.broadcast_to(loss, (H * T8, LANES)).reshape(H, T8, LANES)
    loss_rows = jnp.concatenate([loss_s[h], jnp.zeros((LANES - T8, LANES), f32)], axis=0)
    loss_o[...] = loss_rows.T[0:1, 0:T8]
    for k in range(1, Z):
        recv(f"l4_{k}", dl.at[c, zat(-k)], to_z(-k))
    send("l5", dl.at[c], dl.at[c], to_c)
    recv("l5", dl.at[1 - c], to_c)
    d_logits = jnp.concatenate(
        [dl[0].reshape(Z * H, 1, T8, LANES), dl[1].reshape(Z * H, 1, T8, LANES)], axis=1
    ).reshape(tokens, LANES)

    d_high, d_low = split(d_logits)
    d_units = nt(m_high, d_high) + nt(m_high, d_low) + nt(m_low, d_high)
    gate, up = acc[0:F, :], acc[F : 2 * F, :]
    sig = jax.nn.sigmoid(gate)
    d_gate = d_units * up * sig * (1.0 + gate * (1.0 - sig))
    d_up = d_units * (gate * sig)
    units = units_s[...].astype(bf16)
    product = nn(units, d_high) + nn(units, d_low)
    nred[...] = jnp.concatenate([product, tail], axis=0).reshape(nred.shape)
    sum_start("n", nred, nrx)
    acc[0:F, :] = d_gate
    acc[F : 2 * F, :] = d_up
    d_both = acc[...].astype(bf16)

    order = (2, 3, 1, 0)

    def partial(dx, j):
        g = gat(dx, j)
        grads[(dx % X) * Y + j] = nn(d_both, normed_columns(g)).astype(bf16)

    def slot(dx, j):
        return (dx % X) * Y + j

    for j in order:
        partial(2, j)
        far = grads.at[slot(2, j)]
        send(f"ra{j}", far.at[pl.ds(0, CUT)], ra.at[j], to_x(1))
        send(f"rb{j}", far.at[pl.ds(CUT, 2 * F - CUT)], rb.at[j], to_x(-1))
        partial(1, j)
        partial(-1, j)
        partial(0, j)
    sum_middle("n", nred, nrx, nry)
    for j in order:
        recv(f"ra{j}", ra.at[j], to_x(-1))
        at = slot(1, j)
        joined = grads[at, 0:CUT, :].astype(f32) + ra[j].astype(f32)
        grads[at, 0:CUT, :] = joined.astype(bf16)
        send(f"sp{j}", grads.at[at], sp.at[j], to_x(1))
        recv(f"rb{j}", rb.at[j], to_x(1))
        at = slot(-1, j)
        joined = grads[at, CUT : 2 * F, :].astype(f32) + rb[j].astype(f32)
        grads[at, CUT : 2 * F, :] = joined.astype(bf16)
        send(f"sm{j}", grads.at[at], sm.at[j], to_x(-1))
    sum_spread("n", nred, nrx, nry)
    big_n = None
    for j in order:
        if j == 0:
            big_n = sum_end("n", nred, nrx, nry)
            n_high, n_low = split(big_n)
            gd_o[...] = nn(n_high, head_own[...].astype(bf16)) + nn(n_low, head_own[...].astype(bf16))
        recv(f"sp{j}", sp.at[j], to_x(-1))
        recv(f"sm{j}", sm.at[j], to_x(1))
        at = slot(0, j)
        total = grads[at].astype(f32) + sp[j].astype(f32) + sm[j].astype(f32)
        if j:
            grads[at] = total.astype(bf16)
            send(f"ry{j}", grads.at[at], ry.at[j - 1], to_y(j))
        else:
            acc[:, 0:RB] = total
    for j in (2, 3, 1):
        recv(f"ry{j}", ry.at[j - 1], to_y(j))
    result = acc[:, 0:RB] + ry[0].astype(f32) + ry[1].astype(f32) + ry[2].astype(f32)
    gg_o[...] = result[0:F]
    gu_o[...] = result[F : 2 * F]
    wires.finish()


def solution(mesh):
    Z = mesh.shape["shard"] // (H * C)
    names = wire_names(Z)

    def local(hidden, norm_gain, gate_codes, gate_scales, up_codes, up_scales, down_codes, down_scales, head, teacher, targets):
        T8, D = hidden.shape
        RB, F = gate_codes.shape
        B = head.shape[1]
        tokens = teacher.shape[0]
        KH = D // 2
        chunk = -(-F // (8 * X)) * 8
        vmem = pl.BlockSpec(memory_space=pltpu.VMEM)
        smem = pl.BlockSpec(memory_space=pltpu.SMEM)
        grad = jax.ShapeDtypeStruct((F, RB), f32)
        V = pltpu.VMEM
        scratch = [
            V((2, T8, KH), f32),
            V((2, T8, KH), f32),
            V((2, Z * H, 2 * T8, KH), bf16),
            V((X * Y, 2 * F, RB), bf16),
            V((128, 256), f32),
            V((LANES, RB), f32),
            V((T8, LANES), f32),
            V((LANES, tokens), f32),
            V((tokens // T8, T8, LANES), f32),
            V((2 * F, tokens), f32),
            V((F, tokens), f32),
            V((X, chunk, LANES), f32),
            V((X, chunk, LANES), f32),
            V((X, chunk, LANES), f32),
            V((X + Y, chunk, LANES), f32),
            V((X, chunk, LANES), f32),
            V((X, chunk, LANES), f32),
            V((X + Y, chunk, LANES), f32),
            V((C, Z, H, T8, LANES), f32),
            V((Z, H, T8, LANES), f32),
            V((Z, H, T8, LANES), f32),
            V((Z - 1, H, T8, LANES), f32),
            V((H, T8, LANES), f32),
            V((H, T8, LANES), f32),
            V((C, Z, H, T8, LANES), f32),
            V((H, T8, LANES), f32),
            V((X * Y, 2 * F, RB), bf16),
            V((Y, CUT, RB), bf16),
            V((Y, 2 * F - CUT, RB), bf16),
            V((Y, 2 * F, RB), bf16),
            V((Y, 2 * F, RB), bf16),
            V((Y - 1, 2 * F, RB), bf16),
            pltpu.SemaphoreType.DMA((len(names),)),
            pltpu.SemaphoreType.DMA((len(names),)),
        ]
        loss, gate, up, down = pl.pallas_call(
            functools.partial(kernel, names, Z, D, F, B),
            out_shape=(jax.ShapeDtypeStruct((1, T8), f32), grad, grad, grad),
            in_specs=[vmem] * 10 + [smem],
            out_specs=(vmem,) * 4,
            scratch_shapes=scratch,
            compiler_params=pltpu.CompilerParams(
                collective_id=0, has_side_effects=True, vmem_limit_bytes=50 << 20
            ),
            name="step",
        )(
            hidden, norm_gain.reshape(1, D), gate_codes.T, gate_scales, up_codes.T, up_scales,
            down_codes.T, down_scales, head.T, teacher.T, targets,
        )
        return (loss.reshape(T8), gate.T, up.T, down.T)

    in_specs = (
        P(("grp", "shard"), None),
        P(),
        P("grp", "shard"),
        P("grp", "shard"),
        P("grp", "shard"),
        P("grp", "shard"),
        P("grp", "shard"),
        P("grp", "shard"),
        P(),
        P("grp", None),
        P("grp"),
    )
    out_specs = (P(("grp", "shard")), P("grp", "shard"), P("grp", "shard"), P("grp", "shard"))
    return jax.shard_map(local, mesh=mesh, in_specs=in_specs, out_specs=out_specs, check_vma=False)
```

```python
import functools

import jax
import jax.numpy as jnp
from jax import lax
from jax.experimental import pallas as pl
from jax.experimental.pallas import tpu as pltpu
from jax.sharding import PartitionSpec as P

eps = 1e-05
loss_scale = 64.0
MESH = pl.DeviceIdType.MESH
f32, bf16 = jnp.float32, jnp.bfloat16

X, Y = 4, 4
H, C = 2, 2
CUT = 160
LANES = 128


def nt(left, right):
    return lax.dot_general(left, right, (((1,), (1,)), ((), ())), preferred_element_type=f32)


def nn(left, right):
    return jnp.dot(left, right, preferred_element_type=f32)


def tn(left, right):
    return lax.dot_general(left, right, (((0,), (0,)), ((), ())), preferred_element_type=f32)


def split(value):
    high = value.astype(bf16)
    return high, (value - high.astype(f32)).astype(bf16)


class Wires:
    def __init__(self, send_sems, recv_sems, names):
        self.send_sems, self.recv_sems, self.names, self.started = send_sems, recv_sems, names, []

    def slot(self, name):
        return self.names[name]

    def describe(self, name, src, dst, device):
        at = self.slot(name)
        return pltpu.make_async_remote_copy(
            src_ref=src,
            dst_ref=dst,
            send_sem=self.send_sems.at[at],
            recv_sem=self.recv_sems.at[at],
            device_id=device,
            device_id_type=MESH,
        )

    def send(self, name, src, dst, device):
        copy = self.describe(name, src, dst, device)
        copy.start()
        self.started.append(copy)

    def recv(self, name, dst, device):
        self.describe(name, dst, dst, device).wait_recv()

    def finish(self):
        for copy in self.started:
            copy.wait_send()


def wire_names(Z):
    half = Z // 2
    names = ["e", "hx0", "hx1", "l1", "l3", "l5"]
    for j in range(Y):
        names += [f"{kind}{j}" for kind in ("fp", "fm", "ra", "rb", "sp", "sm", "ry")]
        names += [f"{kind}{p}{j}" for kind in ("y", "xp", "xm") for p in "AB"]
    for s in range(2):
        for n in range(1, half + 1):
            names += [f"z{way}{s}{q}_{n}" for way in "pm" for q in range(2)]
        for k in range(-half, half + 1):
            names.append(f"c{s}_{k}")
    for k in range(1, Z):
        names += [f"l2_{k}", f"l4_{k}"]
    for kind in ("m", "n"):
        for k in range(1, X):
            names += [f"{kind}r{k}", f"{kind}a{k}"]
        for j in range(1, Y):
            names.append(f"{kind}y{j}")
    return {name: at for at, name in enumerate(names)}


def kernel(
    names, Z, D, F, B,
    hid, gain, gc, gs, uc, us, dc, ds, head, teach, targ,
    loss_o, gg_o, gu_o, gd_o,
    halves, pair, nb, wt, scale_pad, head_own, own_logit, teach_pad, teach_rows,
    acc, units_s, whole, mred, mrx, mry, nred, nrx, nry,
    part, l1_in, summed, l2_in, l3_out, l3_in, dl, loss_s,
    grads, ra, rb, sp, sm, ry,
    send_sems, recv_sems,
):
    grp, sh = lax.axis_index("grp"), lax.axis_index("shard")
    x, y = lax.div(grp, Y), lax.rem(grp, Y)
    z, h, c = lax.div(sh, H * C), lax.rem(lax.div(sh, C), H), lax.rem(sh, C)
    half = Z // 2
    RB = D // (X * Y)
    T8 = hid.shape[0]
    KH = D // 2

    def xat(dx):
        return lax.rem(x + dx % X, X) if dx % X else x

    def yat(j):
        return (y, y + 1 - 2 * lax.rem(y, 2), y + 2 - 4 * lax.div(y, 2), 3 - y)[j]

    def zat(dz):
        return lax.rem(z + dz % Z, Z) if dz % Z else z

    def to_x(dx):
        return {"grp": xat(dx) * Y + y}

    def to_y(j):
        return {"grp": x * Y + yat(j)}

    def hat(flip):
        return 1 - h if flip else h

    def to_z(dz, flip=0):
        return {"shard": (zat(dz) * H + hat(flip)) * C + c}

    to_h = to_z(0, 1)
    to_c = {"shard": (z * H + h) * C + (1 - c)}

    wires = Wires(send_sems, recv_sems, names)
    send, recv = wires.send, wires.recv

    barrier = pltpu.get_barrier_semaphore()
    around = sorted(range(1, Z), key=lambda k: -min(k, Z - k))
    peers = [to_z(k) for k in around] + [to_h]
    peers += [to_y(j) for j in range(1, Y)] + [to_x(k) for k in range(1, X)] + [to_c]
    for peer in peers:
        pl.semaphore_signal(barrier, inc=1, device_id=peer, device_id_type=MESH)

    xf = hid[...].astype(f32)
    mean = jnp.mean(xf * xf, axis=1, keepdims=True)
    normed = (xf * lax.rsqrt(mean + eps) * gain[...]).astype(bf16).astype(f32)
    halves[0] = normed[:, :KH]
    halves[1] = normed[:, KH:]
    pair[c] = halves[c]

    scale_pad[...] = jnp.zeros_like(scale_pad)
    scale_pad[0:2, 0:F] = gs[...]
    scale_pad[8:10, 0:F] = us[...]
    scale_pad[16:18, 0:F] = ds[...]
    columns = scale_pad[...].T

    def dequantize(codes, at):
        value = codes[...].astype(f32)
        mid = RB // 2
        left = value[:, :mid] * columns[:F, at : at + 1]
        right = value[:, mid:] * columns[:F, at + 1 : at + 2]
        return jnp.concatenate([left, right], axis=1)

    wt[grp] = jnp.concatenate([dequantize(gc, 0), dequantize(uc, 8)], axis=0).astype(bf16)

    head_own[...] = jnp.zeros_like(head_own)
    head_own[0:B, :] = head[:, pl.ds(pl.multiple_of(grp * RB, RB), RB)].astype(f32)
    head_block = head_own[...].astype(bf16)
    w_down = dequantize(dc, 16).astype(bf16)
    product = nt(w_down, head_block)
    rows = mred.shape[0] * mred.shape[1]
    tail = jnp.zeros((rows - F, LANES), f32)
    mred[...] = jnp.concatenate([product, tail], axis=0).reshape(mred.shape)

    pl.semaphore_wait(barrier, len(peers))

    send("e", halves.at[1 - c], pair.at[c], to_c)
    def gat(dx, j):
        return xat(dx) * Y + yat(j)

    def rows_of(block, p):
        return block.at[pl.ds(0, CUT)] if p == "A" else block.at[pl.ds(CUT, 2 * F - CUT)]

    def pass_on(name, block, device):
        send(name, block, block, device)

    def spread_x(j):
        block = wt.at[gat(0, j)]
        if j:
            recv(f"yA{j}", rows_of(block, "A"), to_y(j))
        if j == 2:
            pass_on("yA3", rows_of(block, "A"), to_y(1))
        pass_on(f"xpA{j}", rows_of(block, "A"), to_x(1))
        if j:
            recv(f"yB{j}", rows_of(block, "B"), to_y(j))
        if j == 2:
            pass_on("yB3", rows_of(block, "B"), to_y(1))
        pass_on(f"xmB{j}", rows_of(block, "B"), to_x(-1))
        pass_on(f"xpB{j}", rows_of(block, "B"), to_x(1))
        pass_on(f"xmA{j}", rows_of(block, "A"), to_x(-1))

    def forward_x(j):
        low, high = rows_of(wt.at[gat(-1, j)], "A"), rows_of(wt.at[gat(1, j)], "B")
        recv(f"xpA{j}", low, to_x(-1))
        pass_on(f"fp{j}", low, to_x(1))
        recv(f"xmB{j}", high, to_x(1))
        pass_on(f"fm{j}", high, to_x(-1))

    def finish_x(j):
        recv(f"xpB{j}", rows_of(wt.at[gat(-1, j)], "B"), to_x(-1))
        recv(f"xmA{j}", rows_of(wt.at[gat(1, j)], "A"), to_x(1))
        opposite = wt.at[gat(2, j)]
        recv(f"fp{j}", rows_of(opposite, "A"), to_x(-1))
        recv(f"fm{j}", rows_of(opposite, "B"), to_x(1))

    def start_y(p, j):
        pass_on(f"y{p}{j}", rows_of(wt.at[grp], p), to_y(j))

    def block_of(s, dz):
        return nb.at[c, zat(dz) * H + (h if s == 0 else 1 - h)]

    def other_block_of(s, dz):
        return nb.at[1 - c, zat(dz) * H + (h if s == 0 else 1 - h)]

    def column_half(ref, at):
        return ref.at[:, pl.ds(at * (KH // 2), KH // 2)]

    def start_z(s):
        block = block_of(s, 0)
        for q in range(2):
            if s:
                recv(f"hx{q}", column_half(block, q), to_h)
            pass_on(f"zp{s}{q}_1", column_half(block, q), to_z(1))
            pass_on(f"zm{s}{q}_1", column_half(block, q), to_z(-1))
        pass_on(f"c{s}_0", block, to_c)

    def step_z(s, n):
        low, high = block_of(s, -n), block_of(s, n)
        for q in range(2):
            if n < half:
                recv(f"zp{s}{q}_{n}", column_half(low, q), to_z(-1))
                if n + 1 < half or q == 0:
                    pass_on(f"zp{s}{q}_{n + 1}", column_half(low, q), to_z(1))
                recv(f"zm{s}{q}_{n}", column_half(high, q), to_z(1))
                if n + 1 < half or q == 1:
                    pass_on(f"zm{s}{q}_{n + 1}", column_half(high, q), to_z(-1))
            elif q == 0:
                recv(f"zp{s}0_{n}", column_half(low, 0), to_z(-1))
            else:
                recv(f"zm{s}1_{n}", column_half(low, 1), to_z(1))
        if n < half:
            pass_on(f"c{s}_{-n}", low, to_c)
        pass_on(f"c{s}_{n}", high, to_c)

    def sum_start(kind, red, rx):
        for k in range(1, X):
            send(f"{kind}r{k}", red.at[xat(k)], rx.at[k - 1], to_x(k))

    def sum_middle(kind, red, rx, ry_):
        for k in range(1, X):
            recv(f"{kind}r{k}", rx.at[k - 1], to_x(-k))
        ry_[0] = red[x] + rx[0] + rx[1] + rx[2]
        for j in range(1, Y):
            send(f"{kind}y{j}", ry_.at[0], ry_.at[j], to_y(j))

    def sum_spread(kind, red, rx, ry_):
        for j in range(1, Y):
            recv(f"{kind}y{j}", ry_.at[j], to_y(j))
        rx[X - 1] = ry_[0] + ry_[1] + ry_[2] + ry_[3]
        for k in range(1, X):
            send(f"{kind}a{k}", rx.at[X - 1], ry_.at[Y + k - 1], to_x(k))

    def sum_end(kind, red, rx, ry_):
        whole[x] = rx[X - 1]
        for k in range(1, X):
            recv(f"{kind}a{k}", ry_.at[Y + k - 1], to_x(-k))
            whole[xat(-k)] = ry_[Y + k - 1]
        return whole[...].reshape(red.shape[0] * red.shape[1], LANES)[:F]

    sum_start("m", mred, mrx)
    spread_x(0)
    start_y("A", 1)
    recv("e", pair.at[1 - c], to_c)
    nb[c, z * H + h] = pair[...].reshape(2 * T8, KH).astype(bf16)
    own = block_of(0, 0)
    for q in range(2):
        pass_on(f"hx{q}", column_half(own, q), to_h)
    start_z(0)
    start_y("B", 1)
    start_y("A", 2)
    start_y("B", 2)

    step_z(0, 1)
    forward_x(0)
    step_z(0, 2)
    start_z(1)
    spread_x(1)
    step_z(0, 3)
    step_z(1, 1)
    spread_x(2)
    step_z(0, 4)
    step_z(1, 2)
    forward_x(1)
    sum_middle("m", mred, mrx, mry)
    step_z(0, 5)
    step_z(1, 3)
    spread_x(3)
    forward_x(2)
    step_z(0, 6)
    step_z(1, 4)
    forward_x(3)
    sum_spread("m", mred, mrx, mry)
    step_z(1, 5)
    step_z(1, 6)
    for j in range(Y):
        finish_x(j)
    for s in range(2):
        for k in range(-half + 1, half + 1):
            recv(f"c{s}_{k}", other_block_of(s, k), to_c)

    tokens = acc.shape[1]
    per = X * Y // 2

    def normed_columns(g):
        at = lax.rem(g, per)
        return nb[lax.div(g, per), :, :, pl.ds(pl.multiple_of(at * RB, RB), RB)].reshape(tokens, RB)

    def add_blocks(at, carry):
        total = acc[...]
        for k in range(4):
            total = total + nt(wt[4 * at + k], normed_columns(4 * at + k))
        acc[...] = total
        return carry

    acc[...] = jnp.zeros_like(acc)
    lax.fori_loop(0, X * Y // 4, add_blocks, 0)
    gate, up = acc[0:F, :], acc[F : 2 * F, :]
    sig = jax.nn.sigmoid(gate)
    units = (gate * sig * up).astype(bf16)
    units_s[...] = units.astype(f32)

    big_m = sum_end("m", mred, mrx, mry)
    m_high, m_low = split(big_m)
    share = (tn(units, m_high) + tn(units, m_low)).reshape(Z * H, C, T8, LANES)
    part[0] = share[:, 0].reshape(Z, H, T8, LANES)
    part[1] = share[:, 1].reshape(Z, H, T8, LANES)
    send("l1", part.at[1 - c], l1_in, to_c)
    recv("l1", l1_in, to_c)
    summed[...] = part[c] + l1_in[...]
    for k in around:
        send(f"l2_{k}", summed.at[zat(k)], l2_in.at[k], to_z(k))

    own_logit[...] = jnp.zeros_like(own_logit)
    own_logit[:, 0:B] = nt(hid[...], head[...])
    teach_pad[...] = jnp.zeros_like(teach_pad)
    teach_pad[0:B, :] = teach[...]
    teach_rows[...] = teach_pad[...].T.reshape(teach_rows.shape)
    lane = lax.broadcasted_iota(jnp.int32, (H * T8, LANES), 1)
    sub = lax.broadcasted_iota(jnp.int32, (H * T8, LANES), 0)
    valid = lane < B
    first = (z * H * C + c) * T8
    wanted = jnp.zeros((H * T8, LANES), jnp.int32)
    for at in range(H * T8):
        value = targ[first + (at // T8) * C * T8 + at % T8]
        wanted = jnp.where(sub == at, value, wanted)
    onehot = jnp.where(lane == wanted, 1.0, 0.0)

    def log_softmax(values):
        top = jnp.max(jnp.where(valid, values, -jnp.inf), axis=1, keepdims=True)
        shifted = jnp.where(valid, values - top, 0.0)
        bottom = jnp.sum(jnp.where(valid, jnp.exp(shifted), 0.0), axis=1, keepdims=True)
        return shifted - jnp.log(bottom)

    teacher = jnp.concatenate([teach_rows[z * H * C + k * C + c] for k in range(H)], axis=0)
    log_teacher = log_softmax(teacher)
    p_teacher = jnp.exp(log_teacher)

    total = summed[z]
    for k in reversed(around):
        recv(f"l2_{k}", l2_in.at[k], to_z(-k))
        total = total + l2_in[k]
    l3_out[...] = total
    l3_out[h] = l3_out[h] + own_logit[...]
    send("l3", l3_out, l3_in, to_h)
    acc[0:F, :] = up * sig * (1.0 + gate * (1.0 - sig))
    acc[F : 2 * F, :] = gate * sig
    recv("l3", l3_in, to_h)
    logits = (l3_out[...] + l3_in[...]).reshape(H * T8, LANES)

    log_student = log_softmax(logits)
    p_student = jnp.exp(log_student)
    d_own = jnp.where(valid, loss_scale * (2.0 * p_student - onehot - p_teacher), 0.0)
    dl[c, z] = d_own.astype(bf16)
    for k in around:
        pass_on(f"l4_{k}", dl.at[c, z], to_z(k))
    terms = jnp.where(valid, p_teacher * (log_teacher - log_student) - onehot * log_student, 0.0)
    loss = jnp.broadcast_to(jnp.sum(terms, axis=1, keepdims=True), (H * T8, LANES))
    loss_s[...] = loss.reshape(H, T8, LANES)
    loss_rows = jnp.concatenate([loss_s[h], jnp.zeros((LANES - T8, LANES), f32)], axis=0)
    loss_o[...] = loss_rows.T[0:1, 0:T8]
    for k in reversed(around):
        recv(f"l4_{k}", dl.at[c, zat(-k)], to_z(-k))
    pass_on("l5", dl.at[c], to_c)
    recv("l5", dl.at[1 - c], to_c)
    d_logits = jnp.concatenate(
        [dl[k].astype(f32).reshape(Z * H, 1, T8, LANES) for k in range(C)], axis=1
    ).reshape(tokens, LANES)

    d_logits = d_logits.astype(bf16)
    d_units = nt(m_high, d_logits) + nt(m_low, d_logits)
    acc[0:F, :] = d_units * acc[0:F, :]
    acc[F : 2 * F, :] = d_units * acc[F : 2 * F, :]
    d_both = acc[...].astype(bf16)


    def partial(dx, j):
        g = gat(dx, j)
        grads[(dx % X) * Y + j] = nn(d_both, normed_columns(g)).astype(bf16)

    def slot(dx, j):
        return (dx % X) * Y + j

    def start_rs(j):
        partial(2, j)
        opposite = grads.at[slot(2, j)]
        send(f"ra{j}", rows_of(opposite, "A"), ra.at[j], to_x(1))
        send(f"rb{j}", rows_of(opposite, "B"), rb.at[j], to_x(-1))

    def join_rs(j):
        partial(1, j)
        recv(f"ra{j}", ra.at[j], to_x(-1))
        at = slot(1, j)
        joined = grads[at, 0:CUT, :].astype(f32) + ra[j].astype(f32)
        grads[at, 0:CUT, :] = joined.astype(bf16)
        send(f"sp{j}", grads.at[at], sp.at[j], to_x(1))
        partial(-1, j)
        recv(f"rb{j}", rb.at[j], to_x(1))
        at = slot(-1, j)
        joined = grads[at, CUT : 2 * F, :].astype(f32) + rb[j].astype(f32)
        grads[at, CUT : 2 * F, :] = joined.astype(bf16)
        send(f"sm{j}", grads.at[at], sm.at[j], to_x(-1))
        partial(0, j)

    def finish_rs(j):
        recv(f"sp{j}", sp.at[j], to_x(-1))
        recv(f"sm{j}", sm.at[j], to_x(1))
        at = slot(0, j)
        total = grads[at].astype(f32) + sp[j].astype(f32) + sm[j].astype(f32)
        if j == 2:
            recv("ry3", ry.at[2], to_y(1))
            total = total + ry[2].astype(f32)
        if j == 0:
            return total
        grads[at] = total.astype(bf16)
        send(f"ry{j}", grads.at[at], ry.at[j - 1], to_y(2 if j == 2 else 1))

    start_rs(3)
    product = nn(units_s[...].astype(bf16), d_logits)
    nred[...] = jnp.concatenate([product, tail], axis=0).reshape(nred.shape)
    sum_start("n", nred, nrx)
    start_rs(2)
    join_rs(3)
    start_rs(1)
    join_rs(2)
    start_rs(0)
    finish_rs(3)
    sum_middle("n", nred, nrx, nry)
    join_rs(1)
    finish_rs(2)
    sum_spread("n", nred, nrx, nry)
    join_rs(0)
    finish_rs(1)
    n_high, n_low = split(sum_end("n", nred, nrx, nry))
    head_block = head_own[...].astype(bf16)
    gd_o[...] = nn(n_high, head_block) + nn(n_low, head_block)
    result = finish_rs(0)
    for j in (1, 2):
        recv(f"ry{j}", ry.at[j - 1], to_y(j))
        result = result + ry[j - 1].astype(f32)
    gg_o[...] = result[0:F]
    gu_o[...] = result[F : 2 * F]
    wires.finish()


def solution(mesh):
    Z = mesh.shape["shard"] // (H * C)
    names = wire_names(Z)

    def local(hidden, norm_gain, gate_codes, gate_scales, up_codes, up_scales, down_codes, down_scales, head, teacher, targets):
        T8, D = hidden.shape
        RB, F = gate_codes.shape
        B = head.shape[1]
        tokens = teacher.shape[0]
        KH = D // 2
        chunk = -(-F // (8 * X)) * 8
        vmem = pl.BlockSpec(memory_space=pltpu.VMEM)
        smem = pl.BlockSpec(memory_space=pltpu.SMEM)
        grad = jax.ShapeDtypeStruct((F, RB), f32)
        V = pltpu.VMEM
        scratch = [
            V((2, T8, KH), f32),
            V((2, T8, KH), f32),
            V((2, Z * H, 2 * T8, KH), bf16),
            V((X * Y, 2 * F, RB), bf16),
            V((128, 256), f32),
            V((LANES, RB), f32),
            V((T8, LANES), f32),
            V((LANES, tokens), f32),
            V((tokens // T8, T8, LANES), f32),
            V((2 * F, tokens), f32),
            V((F, tokens), f32),
            V((X, chunk, LANES), f32),
            V((X, chunk, LANES), f32),
            V((X, chunk, LANES), f32),
            V((X + Y, chunk, LANES), f32),
            V((X, chunk, LANES), f32),
            V((X, chunk, LANES), f32),
            V((X + Y, chunk, LANES), f32),
            V((C, Z, H, T8, LANES), f32),
            V((Z, H, T8, LANES), f32),
            V((Z, H, T8, LANES), f32),
            V((Z, H, T8, LANES), f32),
            V((H, T8, LANES), f32),
            V((H, T8, LANES), f32),
            V((C, Z, H * T8, LANES), bf16),
            V((H, T8, LANES), f32),
            V((X * Y, 2 * F, RB), bf16),
            V((Y, CUT, RB), bf16),
            V((Y, 2 * F - CUT, RB), bf16),
            V((Y, 2 * F, RB), bf16),
            V((Y, 2 * F, RB), bf16),
            V((Y - 1, 2 * F, RB), bf16),
            pltpu.SemaphoreType.DMA((len(names),)),
            pltpu.SemaphoreType.DMA((len(names),)),
        ]
        loss, gate, up, down = pl.pallas_call(
            functools.partial(kernel, names, Z, D, F, B),
            out_shape=(jax.ShapeDtypeStruct((1, T8), f32), grad, grad, grad),
            in_specs=[pl.BlockSpec()] * 10 + [smem],
            out_specs=(vmem,) * 4,
            scratch_shapes=scratch,
            compiler_params=pltpu.CompilerParams(
                collective_id=0, has_side_effects=True, vmem_limit_bytes=62 << 20
            ),
            name="step",
        )(
            hidden, norm_gain.reshape(1, D), gate_codes.T, gate_scales, up_codes.T, up_scales,
            down_codes.T, down_scales, head.T, teacher.T, targets,
        )
        return (loss.reshape(T8), gate.T, up.T, down.T)

    in_specs = (
        P(("grp", "shard"), None),
        P(),
        P("grp", "shard"),
        P("grp", "shard"),
        P("grp", "shard"),
        P("grp", "shard"),
        P("grp", "shard"),
        P("grp", "shard"),
        P(),
        P("grp", None),
        P("grp"),
    )
    out_specs = (P(("grp", "shard")), P("grp", "shard"), P("grp", "shard"), P("grp", "shard"))
    return jax.shard_map(local, mesh=mesh, in_specs=in_specs, out_specs=out_specs, check_vma=False)
```

```python
import functools

import jax
import jax.numpy as jnp
from jax import lax
from jax.experimental import pallas as pl
from jax.experimental.pallas import tpu as pltpu
from jax.sharding import PartitionSpec as P

eps = 1e-05
loss_scale = 64.0
MESH = pl.DeviceIdType.MESH
f32, bf16 = jnp.float32, jnp.bfloat16

X, Y = 4, 4
H, C = 2, 2
REACH = ((0, 1, 1, 1, 1, 1, 1), (0, 1, 1, 1, 1, 1, 0))
CUT = 160
CUT_1 = 240
LANES = 128


def nt(left, right):
    return lax.dot_general(left, right, (((1,), (1,)), ((), ())), preferred_element_type=f32)


def nn(left, right):
    return jnp.dot(left, right, preferred_element_type=f32)


def tn(left, right):
    return lax.dot_general(left, right, (((0,), (0,)), ((), ())), preferred_element_type=f32)


def split(value):
    high = value.astype(bf16)
    return high, (value - high.astype(f32)).astype(bf16)


class Wires:
    def __init__(self, send_sems, recv_sems, names):
        self.send_sems, self.recv_sems, self.names, self.started = send_sems, recv_sems, names, []

    def slot(self, name):
        return self.names[name]

    def describe(self, name, src, dst, device):
        at = self.slot(name)
        return pltpu.make_async_remote_copy(
            src_ref=src,
            dst_ref=dst,
            send_sem=self.send_sems.at[at],
            recv_sem=self.recv_sems.at[at],
            device_id=device,
            device_id_type=MESH,
        )

    def send(self, name, src, dst, device):
        copy = self.describe(name, src, dst, device)
        copy.start()
        self.started.append(copy)

    def recv(self, name, dst, device):
        self.describe(name, dst, dst, device).wait_recv()

    def finish(self):
        for copy in self.started:
            copy.wait_send()


def wire_names(Z):
    half = Z // 2
    names = ["e", "hx0", "hx1", "hy0", "hy1", "l1", "l3", "l5"]
    for j in range(Y):
        names += [f"{kind}{j}" for kind in ("fp", "fm", "ra", "rb", "sp", "sm", "ry", "rq")]
        names += [f"{kind}{p}{j}" for kind in ("y", "xp", "xm") for p in "AB"]
    for s in range(2):
        for n in range(1, half + 1):
            names += [f"z{way}{s}{q}_{n}" for way in "pm" for q in range(2)]
        for k in range(-half, half + 1):
            names.append(f"c{s}_{k}")
    for k in range(1, Z):
        names += [f"l2_{k}", f"l4_{k}"]
    for kind in ("m", "n"):
        for k in range(1, X):
            names += [f"{kind}r{k}", f"{kind}a{k}"]
        for j in range(1, Y):
            names.append(f"{kind}y{j}")
    return {name: at for at, name in enumerate(names)}


def kernel(
    names, Z, D, F, B,
    hid, gain, gc, gs, uc, us, dc, ds, head, teach, targ,
    loss_o, gg_o, gu_o, gd_o,
    halves, pair, nb, wt, scale_pad, head_own, own_logit, teach_pad, teach_rows,
    acc, units_s, whole, mred, mrx, mry, nred, nrx, nry,
    part, l1_in, summed, l2_in, l3_out, l3_in, dl, loss_s,
    grads, ra, rb, sp, sm, ry, rq,
    send_sems, recv_sems,
):
    grp, sh = lax.axis_index("grp"), lax.axis_index("shard")
    x, y = lax.div(grp, Y), lax.rem(grp, Y)
    z, h, c = lax.div(sh, H * C), lax.rem(lax.div(sh, C), H), lax.rem(sh, C)
    half = Z // 2
    RB = D // (X * Y)
    T8 = hid.shape[0]
    KH = D // 2

    def xat(dx):
        return lax.rem(x + dx % X, X) if dx % X else x

    def yat(j):
        return (y, y + 1 - 2 * lax.rem(y, 2), y + 2 - 4 * lax.div(y, 2), 3 - y)[j]

    def zat(dz):
        return lax.rem(z + dz % Z, Z) if dz % Z else z

    def to_x(dx):
        return {"grp": xat(dx) * Y + y}

    def to_y(j):
        return {"grp": x * Y + yat(j)}

    def hat(flip):
        return 1 - h if flip else h

    def to_z(dz, flip=0):
        return {"shard": (zat(dz) * H + hat(flip)) * C + c}

    to_h = to_z(0, 1)
    to_c = {"shard": (z * H + h) * C + (1 - c)}

    wires = Wires(send_sems, recv_sems, names)
    send, recv = wires.send, wires.recv

    barrier = pltpu.get_barrier_semaphore()
    around = sorted(range(1, Z), key=lambda k: -min(k, Z - k))
    peers = [to_z(k) for k in around] + [to_h]
    peers += [to_y(j) for j in range(1, Y)] + [to_x(k) for k in range(1, X)] + [to_c]
    for peer in peers:
        pl.semaphore_signal(barrier, inc=1, device_id=peer, device_id_type=MESH)

    xf = hid[...].astype(f32)
    mean = jnp.mean(xf * xf, axis=1, keepdims=True)
    normed = (xf * lax.rsqrt(mean + eps) * gain[...]).astype(bf16).astype(f32)
    halves[0] = normed[:, :KH]
    halves[1] = normed[:, KH:]
    pair[c] = halves[c]

    pl.semaphore_wait(barrier, len(peers))
    send("e", halves.at[1 - c], pair.at[c], to_c)

    scale_pad[...] = jnp.zeros_like(scale_pad)
    scale_pad[0:2, 0:F] = gs[...]
    scale_pad[8:10, 0:F] = us[...]
    scale_pad[16:18, 0:F] = ds[...]
    columns = scale_pad[...].T

    def dequantize(codes, at):
        value = codes[...].astype(f32)
        mid = RB // 2
        left = value[:, :mid] * columns[:F, at : at + 1]
        right = value[:, mid:] * columns[:F, at + 1 : at + 2]
        return jnp.concatenate([left, right], axis=1)

    wt[grp] = jnp.concatenate([dequantize(gc, 0), dequantize(uc, 8)], axis=0).astype(bf16)

    def gat(dx, j):
        return xat(dx) * Y + yat(j)

    def rows_of(block, p):
        return block.at[pl.ds(0, CUT)] if p == "A" else block.at[pl.ds(CUT, 2 * F - CUT)]

    def pass_on(name, block, device):
        send(name, block, block, device)

    def spread_x(j):
        block = wt.at[gat(0, j)]
        if j:
            recv(f"yA{j}", rows_of(block, "A"), to_y(j))
        if j == 2:
            pass_on("yA3", rows_of(block, "A"), to_y(1))
        pass_on(f"xpA{j}", rows_of(block, "A"), to_x(1))
        if j:
            recv(f"yB{j}", rows_of(block, "B"), to_y(j))
        if j == 2:
            pass_on("yB3", rows_of(block, "B"), to_y(1))
        pass_on(f"xmB{j}", rows_of(block, "B"), to_x(-1))
        pass_on(f"xpB{j}", rows_of(block, "B"), to_x(1))
        pass_on(f"xmA{j}", rows_of(block, "A"), to_x(-1))

    def forward_x(j):
        low, high = rows_of(wt.at[gat(-1, j)], "A"), rows_of(wt.at[gat(1, j)], "B")
        recv(f"xpA{j}", low, to_x(-1))
        pass_on(f"fp{j}", low, to_x(1))
        recv(f"xmB{j}", high, to_x(1))
        pass_on(f"fm{j}", high, to_x(-1))

    def finish_x(j):
        recv(f"xpB{j}", rows_of(wt.at[gat(-1, j)], "B"), to_x(-1))
        recv(f"xmA{j}", rows_of(wt.at[gat(1, j)], "A"), to_x(1))
        opposite = wt.at[gat(2, j)]
        recv(f"fp{j}", rows_of(opposite, "A"), to_x(-1))
        recv(f"fm{j}", rows_of(opposite, "B"), to_x(1))

    def start_y(p, j):
        pass_on(f"y{p}{j}", rows_of(wt.at[grp], p), to_y(j))

    def block_of(s, dz):
        return nb.at[c, zat(dz) * H + (h if s == 0 else 1 - h)]

    def other_block_of(s, dz):
        return nb.at[1 - c, zat(dz) * H + (h if s == 0 else 1 - h)]

    def column_half(ref, at):
        return ref.at[:, pl.ds(at * (KH // 2), KH // 2)]

    def one_way(s, d, q, sign):
        return d < half or (s == 0 and (q == 0) == (sign == 1))

    def next_z(s, d, q):
        for reach in (2, 1):
            for way, sign in (("p", 1), ("m", -1)):
                goal = d + reach
                if goal <= half and REACH[s][goal] == reach and one_way(s, goal, q, sign):
                    block = column_half(block_of(s, -sign * d), q)
                    pass_on(f"z{way}{s}{q}_{goal}", block, to_z(sign * reach))

    def start_z(s):
        for q in range(2):
            if s:
                recv(f"hx{q}", column_half(block_of(s, 0), q), to_h)
            next_z(s, 0, q)
        pass_on(f"c{s}_0", block_of(s, 0), to_c)

    def step_z(s, d):
        for q in range(2):
            block = column_half(block_of(s, half), q)
            if s == 1 and d == half:
                recv(f"hy{q}", block, to_h)
            for way, sign in (("p", 1), ("m", -1)):
                if one_way(s, d, q, sign):
                    recv(f"z{way}{s}{q}_{d}", column_half(block_of(s, -sign * d), q), to_z(-sign * REACH[s][d]))
            if s == 0 and d == half:
                pass_on(f"hy{q}", block, to_h)
            if d < half:
                next_z(s, d, q)
        if d < half:
            pass_on(f"c{s}_{-d}", block_of(s, -d), to_c)
        pass_on(f"c{s}_{d}", block_of(s, d), to_c)

    def sum_start(kind, red, rx):
        for k in range(1, X):
            send(f"{kind}r{k}", red.at[xat(k)], rx.at[k - 1], to_x(k))

    def sum_middle(kind, red, rx, ry_):
        for k in range(1, X):
            recv(f"{kind}r{k}", rx.at[k - 1], to_x(-k))
        ry_[0] = red[x] + rx[0] + rx[1] + rx[2]
        for j in range(1, Y):
            send(f"{kind}y{j}", ry_.at[0], ry_.at[j], to_y(j))

    def sum_spread(kind, red, rx, ry_):
        for j in range(1, Y):
            recv(f"{kind}y{j}", ry_.at[j], to_y(j))
        rx[X - 1] = ry_[0] + ry_[1] + ry_[2] + ry_[3]
        for k in range(1, X):
            send(f"{kind}a{k}", rx.at[X - 1], ry_.at[Y + k - 1], to_x(k))

    def sum_end(kind, red, rx, ry_):
        whole[x] = rx[X - 1]
        for k in range(1, X):
            recv(f"{kind}a{k}", ry_.at[Y + k - 1], to_x(-k))
            whole[xat(-k)] = ry_[Y + k - 1]
        return whole[...].reshape(red.shape[0] * red.shape[1], LANES)[:F]

    recv("e", pair.at[1 - c], to_c)
    nb[c, z * H + h] = pair[...].reshape(2 * T8, KH).astype(bf16)
    own = block_of(0, 0)
    for q in range(2):
        pass_on(f"hx{q}", column_half(own, q), to_h)
    start_z(0)
    spread_x(0)
    for j in (1, 2):
        for p in "AB":
            start_y(p, j)

    head_own[...] = jnp.zeros_like(head_own)
    head_own[0:B, :] = head[:, pl.ds(pl.multiple_of(grp * RB, RB), RB)].astype(f32)
    head_block = head_own[...].astype(bf16)
    w_down = dequantize(dc, 16).astype(bf16)
    product = nt(w_down, head_block)
    rows = mred.shape[0] * mred.shape[1]
    tail = jnp.zeros((rows - F, LANES), f32)
    mred[...] = jnp.concatenate([product, tail], axis=0).reshape(mred.shape)
    sum_start("m", mred, mrx)

    step_z(0, 1)
    forward_x(0)
    step_z(0, 2)
    start_z(1)
    spread_x(1)
    step_z(0, 3)
    step_z(1, 1)
    spread_x(2)
    step_z(0, 4)
    step_z(1, 2)
    forward_x(1)
    step_z(0, 5)
    step_z(1, 3)
    spread_x(3)
    forward_x(2)
    sum_middle("m", mred, mrx, mry)
    step_z(0, 6)
    step_z(1, 4)
    forward_x(3)
    sum_spread("m", mred, mrx, mry)
    step_z(1, 5)
    step_z(1, 6)
    for j in range(Y):
        finish_x(j)
    for s in range(2):
        for k in range(-half + 1, half + 1):
            recv(f"c{s}_{k}", other_block_of(s, k), to_c)

    tokens = acc.shape[1]
    per = X * Y // 2

    def normed_columns(g):
        at = lax.rem(g, per)
        return nb[lax.div(g, per), :, :, pl.ds(pl.multiple_of(at * RB, RB), RB)].reshape(tokens, RB)

    def add_blocks(at, carry):
        total = acc[...]
        for k in range(4):
            total = total + nt(wt[4 * at + k], normed_columns(4 * at + k))
        acc[...] = total
        return carry

    acc[...] = jnp.zeros_like(acc)
    lax.fori_loop(0, X * Y // 4, add_blocks, 0)
    gate, up = acc[0:F, :], acc[F : 2 * F, :]
    sig = jax.nn.sigmoid(gate)
    units = (gate * sig * up).astype(bf16)
    units_s[...] = units.astype(f32)

    big_m = sum_end("m", mred, mrx, mry)
    m_high, m_low = split(big_m)
    share = (tn(units, m_high) + tn(units, m_low)).reshape(Z * H, C, T8, LANES)
    part[0] = share[:, 0].reshape(Z, H, T8, LANES)
    part[1] = share[:, 1].reshape(Z, H, T8, LANES)
    send("l1", part.at[1 - c], l1_in, to_c)
    recv("l1", l1_in, to_c)
    summed[...] = part[c] + l1_in[...]
    for k in around:
        send(f"l2_{k}", summed.at[zat(k)], l2_in.at[k], to_z(k))

    own_logit[...] = jnp.zeros_like(own_logit)
    own_logit[:, 0:B] = nt(hid[...], head[...])
    teach_pad[...] = jnp.zeros_like(teach_pad)
    teach_pad[0:B, :] = teach[...]
    teach_rows[...] = teach_pad[...].T.reshape(teach_rows.shape)
    lane = lax.broadcasted_iota(jnp.int32, (H * T8, LANES), 1)
    sub = lax.broadcasted_iota(jnp.int32, (H * T8, LANES), 0)
    valid = lane < B
    first = (z * H * C + c) * T8
    wanted = jnp.zeros((H * T8, LANES), jnp.int32)
    for at in range(H * T8):
        value = targ[first + (at // T8) * C * T8 + at % T8]
        wanted = jnp.where(sub == at, value, wanted)
    onehot = jnp.where(lane == wanted, 1.0, 0.0)

    def log_softmax(values):
        top = jnp.max(jnp.where(valid, values, -jnp.inf), axis=1, keepdims=True)
        shifted = jnp.where(valid, values - top, 0.0)
        bottom = jnp.sum(jnp.where(valid, jnp.exp(shifted), 0.0), axis=1, keepdims=True)
        return shifted - jnp.log(bottom)

    teacher = jnp.concatenate([teach_rows[z * H * C + k * C + c] for k in range(H)], axis=0)
    log_teacher = log_softmax(teacher)
    p_teacher = jnp.exp(log_teacher)

    total = summed[z]
    for k in reversed(around):
        recv(f"l2_{k}", l2_in.at[k], to_z(-k))
        total = total + l2_in[k]
    l3_out[...] = total
    l3_out[h] = l3_out[h] + own_logit[...]
    send("l3", l3_out, l3_in, to_h)
    acc[0:F, :] = up * sig * (1.0 + gate * (1.0 - sig))
    acc[F : 2 * F, :] = gate * sig
    recv("l3", l3_in, to_h)
    logits = (l3_out[...] + l3_in[...]).reshape(H * T8, LANES)

    log_student = log_softmax(logits)
    p_student = jnp.exp(log_student)
    d_own = jnp.where(valid, loss_scale * (2.0 * p_student - onehot - p_teacher), 0.0)
    dl[c, z] = d_own.astype(bf16)
    for k in around:
        pass_on(f"l4_{k}", dl.at[c, z], to_z(k))
    terms = jnp.where(valid, p_teacher * (log_teacher - log_student) - onehot * log_student, 0.0)
    loss = jnp.broadcast_to(jnp.sum(terms, axis=1, keepdims=True), (H * T8, LANES))
    loss_s[...] = loss.reshape(H, T8, LANES)
    loss_rows = jnp.concatenate([loss_s[h], jnp.zeros((LANES - T8, LANES), f32)], axis=0)
    loss_o[...] = loss_rows.T[0:1, 0:T8]
    for k in reversed(around):
        recv(f"l4_{k}", dl.at[c, zat(-k)], to_z(-k))
    pass_on("l5", dl.at[c], to_c)
    recv("l5", dl.at[1 - c], to_c)
    d_logits = jnp.concatenate(
        [dl[k].astype(f32).reshape(Z * H, 1, T8, LANES) for k in range(C)], axis=1
    ).reshape(tokens, LANES)

    d_logits = d_logits.astype(bf16)
    d_units = nt(m_high, d_logits) + nt(m_low, d_logits)
    acc[0:F, :] = d_units * acc[0:F, :]
    acc[F : 2 * F, :] = d_units * acc[F : 2 * F, :]
    d_both = acc[...].astype(bf16)

    ends = {j: ((CUT, CUT_1) if j == 1 else (0, CUT)) for j in range(Y)}

    def partial(dx, j):
        g = gat(dx, j)
        grads[(dx % X) * Y + j] = nn(d_both, normed_columns(g)).astype(bf16)

    def slot(dx, j):
        return (dx % X) * Y + j

    def piece(ref, first, last):
        return ref.at[pl.ds(first, last - first)]

    def early_rs():
        for dx in (2, 1, -1, 0):
            partial(dx, 1)
            send(f"rq{dx % X}", piece(grads.at[slot(dx, 1)], 0, CUT), rq.at[dx % X], to_y(1))

    def take_early(dx):
        recv(f"rq{dx % X}", rq.at[dx % X], to_y(1))
        at = slot(dx, 0)
        grads[at, 0:CUT, :] = (grads[at, 0:CUT, :].astype(f32) + rq[dx % X].astype(f32)).astype(bf16)

    def fill(dx, j):
        if j != 1:
            partial(dx, j)
        if j == 0:
            take_early(dx)

    def start_rs(j):
        first, mid = ends[j]
        fill(2, j)
        opposite = grads.at[slot(2, j)]
        send(f"ra{j}", piece(opposite, first, mid), piece(ra.at[j], 0, mid - first), to_x(1))
        send(f"rb{j}", piece(opposite, mid, 2 * F), piece(rb.at[j], 0, 2 * F - mid), to_x(-1))

    def join_rs(j):
        first, mid = ends[j]
        fill(1, j)
        recv(f"ra{j}", piece(ra.at[j], 0, mid - first), to_x(-1))
        at = slot(1, j)
        joined = grads[at, first:mid, :].astype(f32) + ra[j, 0 : mid - first, :].astype(f32)
        grads[at, first:mid, :] = joined.astype(bf16)
        send(f"sp{j}", piece(grads.at[at], first, 2 * F), piece(sp.at[j], first, 2 * F), to_x(1))
        fill(-1, j)
        recv(f"rb{j}", piece(rb.at[j], 0, 2 * F - mid), to_x(1))
        at = slot(-1, j)
        joined = grads[at, mid : 2 * F, :].astype(f32) + rb[j, 0 : 2 * F - mid, :].astype(f32)
        grads[at, mid : 2 * F, :] = joined.astype(bf16)
        send(f"sm{j}", piece(grads.at[at], first, 2 * F), piece(sm.at[j], first, 2 * F), to_x(-1))
        fill(0, j)

    def finish_rs(j):
        first, mid = ends[j]
        recv(f"sp{j}", piece(sp.at[j], first, 2 * F), to_x(-1))
        recv(f"sm{j}", piece(sm.at[j], first, 2 * F), to_x(1))
        at = slot(0, j)
        rows_j = slice(first, 2 * F)
        total = grads[at, rows_j, :].astype(f32) + sp[j, rows_j, :].astype(f32) + sm[j, rows_j, :].astype(f32)
        if j == 2:
            recv("ry3", ry.at[2], to_y(1))
            total = total + ry[2].astype(f32)
        if j == 0:
            return total
        grads[at, rows_j, :] = total.astype(bf16)
        send(f"ry{j}", piece(grads.at[at], first, 2 * F), piece(ry.at[j - 1], first, 2 * F), to_y(2 if j == 2 else 1))

    start_rs(3)
    early_rs()
    start_rs(2)
    product = nn(units_s[...].astype(bf16), d_logits)
    nred[...] = jnp.concatenate([product, tail], axis=0).reshape(nred.shape)
    sum_start("n", nred, nrx)
    join_rs(3)
    start_rs(1)
    join_rs(2)
    start_rs(0)
    finish_rs(3)
    join_rs(1)
    sum_middle("n", nred, nrx, nry)
    finish_rs(2)
    join_rs(0)
    sum_spread("n", nred, nrx, nry)
    finish_rs(1)
    n_high, n_low = split(sum_end("n", nred, nrx, nry))
    head_block = head_own[...].astype(bf16)
    gd_o[...] = nn(n_high, head_block) + nn(n_low, head_block)
    acc[:, 0:RB] = finish_rs(0)
    recv("ry2", ry.at[1], to_y(2))
    acc[:, 0:RB] += ry[1].astype(f32)
    recv("ry1", piece(ry.at[0], CUT, 2 * F), to_y(1))
    acc[CUT : 2 * F, 0:RB] += ry[0, CUT : 2 * F, :].astype(f32)
    gg_o[...] = acc[0:F, 0:RB]
    gu_o[...] = acc[F : 2 * F, 0:RB]
    wires.finish()


def solution(mesh):
    Z = mesh.shape["shard"] // (H * C)
    names = wire_names(Z)

    def local(hidden, norm_gain, gate_codes, gate_scales, up_codes, up_scales, down_codes, down_scales, head, teacher, targets):
        T8, D = hidden.shape
        RB, F = gate_codes.shape
        B = head.shape[1]
        tokens = teacher.shape[0]
        KH = D // 2
        chunk = -(-F // (8 * X)) * 8
        vmem = pl.BlockSpec(memory_space=pltpu.VMEM)
        smem = pl.BlockSpec(memory_space=pltpu.SMEM)
        grad = jax.ShapeDtypeStruct((F, RB), f32)
        V = pltpu.VMEM
        scratch = [
            V((2, T8, KH), f32),
            V((2, T8, KH), f32),
            V((2, Z * H, 2 * T8, KH), bf16),
            V((X * Y, 2 * F, RB), bf16),
            V((128, 256), f32),
            V((LANES, RB), f32),
            V((T8, LANES), f32),
            V((LANES, tokens), f32),
            V((tokens // T8, T8, LANES), f32),
            V((2 * F, tokens), f32),
            V((F, tokens), f32),
            V((X, chunk, LANES), f32),
            V((X, chunk, LANES), f32),
            V((X, chunk, LANES), f32),
            V((X + Y, chunk, LANES), f32),
            V((X, chunk, LANES), f32),
            V((X, chunk, LANES), f32),
            V((X + Y, chunk, LANES), f32),
            V((C, Z, H, T8, LANES), f32),
            V((Z, H, T8, LANES), f32),
            V((Z, H, T8, LANES), f32),
            V((Z, H, T8, LANES), f32),
            V((H, T8, LANES), f32),
            V((H, T8, LANES), f32),
            V((C, Z, H * T8, LANES), bf16),
            V((H, T8, LANES), f32),
            V((X * Y, 2 * F, RB), bf16),
            V((Y, CUT, RB), bf16),
            V((Y, 2 * F - CUT, RB), bf16),
            V((Y, 2 * F, RB), bf16),
            V((Y, 2 * F, RB), bf16),
            V((Y - 1, 2 * F, RB), bf16),
            V((X, CUT, RB), bf16),
            pltpu.SemaphoreType.DMA((len(names),)),
            pltpu.SemaphoreType.DMA((len(names),)),
        ]
        loss, gate, up, down = pl.pallas_call(
            functools.partial(kernel, names, Z, D, F, B),
            out_shape=(jax.ShapeDtypeStruct((1, T8), f32), grad, grad, grad),
            in_specs=[pl.BlockSpec()] * 10 + [smem],
            out_specs=(vmem,) * 4,
            scratch_shapes=scratch,
            compiler_params=pltpu.CompilerParams(
                collective_id=0, has_side_effects=True, vmem_limit_bytes=62 << 20
            ),
            name="step",
        )(
            hidden, norm_gain.reshape(1, D), gate_codes.T, gate_scales, up_codes.T, up_scales,
            down_codes.T, down_scales, head.T, teacher.T, targets,
        )
        return (loss.reshape(T8), gate.T, up.T, down.T)

    in_specs = (
        P(("grp", "shard"), None),
        P(),
        P("grp", "shard"),
        P("grp", "shard"),
        P("grp", "shard"),
        P("grp", "shard"),
        P("grp", "shard"),
        P("grp", "shard"),
        P(),
        P("grp", None),
        P("grp"),
    )
    out_specs = (P(("grp", "shard")), P("grp", "shard"), P("grp", "shard"), P("grp", "shard"))
    return jax.shard_map(local, mesh=mesh, in_specs=in_specs, out_specs=out_specs, check_vma=False)
```

```python
import functools

import jax
import jax.numpy as jnp
from jax import lax
from jax.experimental import pallas as pl
from jax.experimental.pallas import tpu as pltpu
from jax.sharding import PartitionSpec as P

eps = 1e-05
loss_scale = 64.0
MESH = pl.DeviceIdType.MESH
f32, bf16 = jnp.float32, jnp.bfloat16

X, Y = 4, 4
H, C = 2, 2
REACH = ((0, 1, 1, 1, 1, 1, 1), (0, 1, 1, 1, 1, 1, 0))
CUT = 160
CUT_1 = 240
LANES = 128


def nt(left, right):
    return lax.dot_general(left, right, (((1,), (1,)), ((), ())), preferred_element_type=f32)


def nn(left, right):
    return jnp.dot(left, right, preferred_element_type=f32)


def tn(left, right):
    return lax.dot_general(left, right, (((0,), (0,)), ((), ())), preferred_element_type=f32)


def split(value):
    high = value.astype(bf16)
    return high, (value - high.astype(f32)).astype(bf16)


class Wires:
    def __init__(self, send_sems, recv_sems, names):
        self.send_sems, self.recv_sems, self.names, self.started = send_sems, recv_sems, names, []

    def slot(self, name):
        return self.names[name]

    def describe(self, name, src, dst, device):
        at = self.slot(name)
        return pltpu.make_async_remote_copy(
            src_ref=src,
            dst_ref=dst,
            send_sem=self.send_sems.at[at],
            recv_sem=self.recv_sems.at[at],
            device_id=device,
            device_id_type=MESH,
        )

    def send(self, name, src, dst, device):
        copy = self.describe(name, src, dst, device)
        copy.start()
        self.started.append(copy)

    def recv(self, name, dst, device):
        self.describe(name, dst, dst, device).wait_recv()

    def finish(self):
        for copy in self.started:
            copy.wait_send()


def wire_names(Z):
    half = Z // 2
    names = ["e", "hx0", "hx1", "hy0", "hy1", "l1", "l3", "l5"]
    for j in range(Y):
        names += [f"{kind}{j}" for kind in ("fp", "fm", "ra", "rb", "sp", "sm", "ry", "rq")]
        names += [f"{kind}{p}{j}" for kind in ("y", "xp", "xm") for p in "AB"]
    for s in range(2):
        for n in range(1, half + 1):
            names += [f"z{way}{s}{q}_{n}" for way in "pm" for q in range(2)]
        for k in range(-half, half + 1):
            names.append(f"c{s}_{k}")
    for k in range(1, Z):
        names += [f"l2_{k}", f"l4_{k}"]
    for kind in ("m", "n"):
        for k in range(1, X):
            names += [f"{kind}r{k}", f"{kind}a{k}"]
        for j in range(1, Y):
            names.append(f"{kind}y{j}")
    return {name: at for at, name in enumerate(names)}


def kernel(
    names, Z, D, F, B,
    hid, gain, gc, gs, uc, us, dc, ds, head, teach, targ,
    loss_o, gg_o, gu_o, gd_o,
    halves, pair, nb, wt, scale_pad, head_own, own_logit, teach_pad, teach_rows,
    acc, units_s, whole, mred, mrx, mry, nred, nrx, nry,
    part, l1_in, summed, l2_in, l3_out, l3_in, dl, loss_s,
    grads, ra, rb, sp, sm, ry, rq,
    send_sems, recv_sems,
):
    grp, sh = lax.axis_index("grp"), lax.axis_index("shard")
    x, y = lax.div(grp, Y), lax.rem(grp, Y)
    z, h, c = lax.div(sh, H * C), lax.rem(lax.div(sh, C), H), lax.rem(sh, C)
    half = Z // 2
    RB = D // (X * Y)
    T8 = hid.shape[0]
    KH = D // 2

    def xat(dx):
        return lax.rem(x + dx % X, X) if dx % X else x

    def yat(j):
        return (y, y + 1 - 2 * lax.rem(y, 2), y + 2 - 4 * lax.div(y, 2), 3 - y)[j]

    def zat(dz):
        return lax.rem(z + dz % Z, Z) if dz % Z else z

    def to_x(dx):
        return {"grp": xat(dx) * Y + y}

    def to_y(j):
        return {"grp": x * Y + yat(j)}

    def hat(flip):
        return 1 - h if flip else h

    def to_z(dz, flip=0):
        return {"shard": (zat(dz) * H + hat(flip)) * C + c}

    to_h = to_z(0, 1)
    to_c = {"shard": (z * H + h) * C + (1 - c)}

    wires = Wires(send_sems, recv_sems, names)
    send, recv = wires.send, wires.recv

    barrier = pltpu.get_barrier_semaphore()
    around = sorted(range(1, Z), key=lambda k: -min(k, Z - k))
    peers = [to_z(k) for k in around] + [to_h]
    peers += [to_y(j) for j in range(1, Y)] + [to_x(k) for k in range(1, X)] + [to_c]
    for peer in peers:
        pl.semaphore_signal(barrier, inc=1, device_id=peer, device_id_type=MESH)

    xf = hid[...].astype(f32)
    mean = jnp.mean(xf * xf, axis=1, keepdims=True)
    normed = (xf * lax.rsqrt(mean + eps) * gain[...]).astype(bf16).astype(f32)
    halves[0] = normed[:, :KH]
    halves[1] = normed[:, KH:]
    pair[c] = halves[c]

    pl.semaphore_wait(barrier, len(peers))
    send("e", halves.at[1 - c], pair.at[c], to_c)

    scale_pad[...] = jnp.zeros_like(scale_pad)
    scale_pad[0:2, 0:F] = gs[...]
    scale_pad[8:10, 0:F] = us[...]
    scale_pad[16:18, 0:F] = ds[...]
    columns = scale_pad[...].T

    def dequantize(codes, at):
        value = codes[...].astype(f32)
        mid = RB // 2
        left = value[:, :mid] * columns[:F, at : at + 1]
        right = value[:, mid:] * columns[:F, at + 1 : at + 2]
        return jnp.concatenate([left, right], axis=1)

    wt[grp] = jnp.concatenate([dequantize(gc, 0), dequantize(uc, 8)], axis=0).astype(bf16)

    def gat(dx, j):
        return xat(dx) * Y + yat(j)

    def rows_of(block, p):
        return block.at[pl.ds(0, CUT)] if p == "A" else block.at[pl.ds(CUT, 2 * F - CUT)]

    def pass_on(name, block, device):
        send(name, block, block, device)

    def spread_x(j):
        block = wt.at[gat(0, j)]
        if j:
            recv(f"yA{j}", rows_of(block, "A"), to_y(j))
        if j == 2:
            pass_on("yA3", rows_of(block, "A"), to_y(1))
        pass_on(f"xpA{j}", rows_of(block, "A"), to_x(1))
        if j:
            recv(f"yB{j}", rows_of(block, "B"), to_y(j))
        if j == 2:
            pass_on("yB3", rows_of(block, "B"), to_y(1))
        pass_on(f"xmB{j}", rows_of(block, "B"), to_x(-1))
        pass_on(f"xpB{j}", rows_of(block, "B"), to_x(1))
        pass_on(f"xmA{j}", rows_of(block, "A"), to_x(-1))

    def forward_x(j):
        low, high = rows_of(wt.at[gat(-1, j)], "A"), rows_of(wt.at[gat(1, j)], "B")
        recv(f"xpA{j}", low, to_x(-1))
        pass_on(f"fp{j}", low, to_x(1))
        recv(f"xmB{j}", high, to_x(1))
        pass_on(f"fm{j}", high, to_x(-1))

    def finish_x(j):
        recv(f"xpB{j}", rows_of(wt.at[gat(-1, j)], "B"), to_x(-1))
        recv(f"xmA{j}", rows_of(wt.at[gat(1, j)], "A"), to_x(1))
        opposite = wt.at[gat(2, j)]
        recv(f"fp{j}", rows_of(opposite, "A"), to_x(-1))
        recv(f"fm{j}", rows_of(opposite, "B"), to_x(1))

    def start_y(p, j):
        pass_on(f"y{p}{j}", rows_of(wt.at[grp], p), to_y(j))

    def block_of(s, dz):
        return nb.at[c, zat(dz) * H + (h if s == 0 else 1 - h)]

    def other_block_of(s, dz):
        return nb.at[1 - c, zat(dz) * H + (h if s == 0 else 1 - h)]

    def column_half(ref, at):
        return ref.at[:, pl.ds(at * (KH // 2), KH // 2)]

    def one_way(s, d, q, sign):
        return d < half or (s == 0 and (q == 0) == (sign == 1))

    def next_z(s, d, q):
        for reach in (2, 1):
            for way, sign in (("p", 1), ("m", -1)):
                goal = d + reach
                if goal <= half and REACH[s][goal] == reach and one_way(s, goal, q, sign):
                    block = column_half(block_of(s, -sign * d), q)
                    pass_on(f"z{way}{s}{q}_{goal}", block, to_z(sign * reach))

    def start_z(s):
        for q in range(2):
            if s:
                recv(f"hx{q}", column_half(block_of(s, 0), q), to_h)
            next_z(s, 0, q)
        pass_on(f"c{s}_0", block_of(s, 0), to_c)

    def step_z(s, d):
        for q in range(2):
            block = column_half(block_of(s, half), q)
            if s == 1 and d == half:
                recv(f"hy{q}", block, to_h)
            for way, sign in (("p", 1), ("m", -1)):
                if one_way(s, d, q, sign):
                    recv(f"z{way}{s}{q}_{d}", column_half(block_of(s, -sign * d), q), to_z(-sign * REACH[s][d]))
            if s == 0 and d == half:
                pass_on(f"hy{q}", block, to_h)
            if d < half:
                next_z(s, d, q)
        if d < half:
            pass_on(f"c{s}_{-d}", block_of(s, -d), to_c)
        pass_on(f"c{s}_{d}", block_of(s, d), to_c)

    def sum_start(kind, red, rx):
        for k in range(1, X):
            send(f"{kind}r{k}", red.at[xat(k)], rx.at[k - 1], to_x(k))

    def sum_middle(kind, red, rx, ry_):
        for k in range(1, X):
            recv(f"{kind}r{k}", rx.at[k - 1], to_x(-k))
        ry_[0] = red[x] + rx[0] + rx[1] + rx[2]
        for j in range(1, Y):
            send(f"{kind}y{j}", ry_.at[0], ry_.at[j], to_y(j))

    def sum_spread(kind, red, rx, ry_):
        for j in range(1, Y):
            recv(f"{kind}y{j}", ry_.at[j], to_y(j))
        rx[X - 1] = ry_[0] + ry_[1] + ry_[2] + ry_[3]
        for k in range(1, X):
            send(f"{kind}a{k}", rx.at[X - 1], ry_.at[Y + k - 1], to_x(k))

    def sum_end(kind, red, rx, ry_):
        whole[x] = rx[X - 1]
        for k in range(1, X):
            recv(f"{kind}a{k}", ry_.at[Y + k - 1], to_x(-k))
            whole[xat(-k)] = ry_[Y + k - 1]
        return whole[...].reshape(red.shape[0] * red.shape[1], LANES)[:F]

    recv("e", pair.at[1 - c], to_c)
    nb[c, z * H + h] = pair[...].reshape(2 * T8, KH).astype(bf16)
    own = block_of(0, 0)
    for q in range(2):
        pass_on(f"hx{q}", column_half(own, q), to_h)
    start_z(0)
    spread_x(0)
    for j in (1, 2):
        for p in "AB":
            start_y(p, j)

    head_own[...] = jnp.zeros_like(head_own)
    head_own[0:B, :] = head[:, pl.ds(pl.multiple_of(grp * RB, RB), RB)].astype(f32)
    head_block = head_own[...].astype(bf16)
    w_down = dequantize(dc, 16).astype(bf16)
    product = nt(w_down, head_block)
    rows = mred.shape[0] * mred.shape[1]
    tail = jnp.zeros((rows - F, LANES), f32)
    mred[...] = jnp.concatenate([product, tail], axis=0).reshape(mred.shape)
    sum_start("m", mred, mrx)

    step_z(0, 1)
    forward_x(0)
    step_z(0, 2)
    start_z(1)
    spread_x(1)
    step_z(0, 3)
    step_z(1, 1)
    spread_x(2)
    step_z(0, 4)
    step_z(1, 2)
    forward_x(1)
    step_z(0, 5)
    step_z(1, 3)
    spread_x(3)
    forward_x(2)
    sum_middle("m", mred, mrx, mry)
    step_z(0, 6)
    step_z(1, 4)
    forward_x(3)
    sum_spread("m", mred, mrx, mry)
    step_z(1, 5)
    step_z(1, 6)
    for j in range(Y):
        finish_x(j)
    for s in range(2):
        for k in range(-half + 1, half + 1):
            recv(f"c{s}_{k}", other_block_of(s, k), to_c)

    tokens = acc.shape[1]
    per = X * Y // 2

    def normed_columns(g):
        at = lax.rem(g, per)
        return nb[lax.div(g, per), :, :, pl.ds(pl.multiple_of(at * RB, RB), RB)].reshape(tokens, RB)

    def add_blocks(at, carry):
        total = acc[...]
        for k in range(4):
            total = total + nt(wt[4 * at + k], normed_columns(4 * at + k))
        acc[...] = total
        return carry

    acc[...] = jnp.zeros_like(acc)
    lax.fori_loop(0, X * Y // 4, add_blocks, 0)
    gate, up = acc[0:F, :], acc[F : 2 * F, :]
    sig = jax.nn.sigmoid(gate)
    units = (gate * sig * up).astype(bf16)
    units_s[...] = units.astype(f32)

    big_m = sum_end("m", mred, mrx, mry)
    m_high, m_low = split(big_m)
    share = (tn(units, m_high) + tn(units, m_low)).reshape(Z * H, C, T8, LANES)
    part[0] = share[:, 0].reshape(Z, H, T8, LANES)
    part[1] = share[:, 1].reshape(Z, H, T8, LANES)
    send("l1", part.at[1 - c], l1_in, to_c)
    recv("l1", l1_in, to_c)
    shares = part[c] + l1_in[...]
    summed[...] = shares.reshape(Z, H * T8, LANES).astype(bf16)
    for k in around:
        send(f"l2_{k}", summed.at[zat(k)], l2_in.at[k], to_z(k))

    own_logit[...] = jnp.zeros_like(own_logit)
    own_logit[:, 0:B] = nt(hid[...], head[...])
    teach_pad[...] = jnp.zeros_like(teach_pad)
    teach_pad[0:B, :] = teach[...]
    teach_rows[...] = teach_pad[...].T.reshape(teach_rows.shape)
    lane = lax.broadcasted_iota(jnp.int32, (H * T8, LANES), 1)
    sub = lax.broadcasted_iota(jnp.int32, (H * T8, LANES), 0)
    valid = lane < B
    first = (z * H * C + c) * T8
    wanted = jnp.zeros((H * T8, LANES), jnp.int32)
    for at in range(H * T8):
        value = targ[first + (at // T8) * C * T8 + at % T8]
        wanted = jnp.where(sub == at, value, wanted)
    onehot = jnp.where(lane == wanted, 1.0, 0.0)

    def log_softmax(values):
        top = jnp.max(jnp.where(valid, values, -jnp.inf), axis=1, keepdims=True)
        shifted = jnp.where(valid, values - top, 0.0)
        bottom = jnp.sum(jnp.where(valid, jnp.exp(shifted), 0.0), axis=1, keepdims=True)
        return shifted - jnp.log(bottom)

    teacher = jnp.concatenate([teach_rows[z * H * C + k * C + c] for k in range(H)], axis=0)
    log_teacher = log_softmax(teacher)
    p_teacher = jnp.exp(log_teacher)

    total = summed[z].astype(f32)
    for k in reversed(around):
        recv(f"l2_{k}", l2_in.at[k], to_z(-k))
        total = total + l2_in[k].astype(f32)
    l3_out[...] = total.reshape(H, T8, LANES)
    l3_out[h] = l3_out[h] + own_logit[...]
    send("l3", l3_out, l3_in, to_h)
    acc[0:F, :] = up * sig * (1.0 + gate * (1.0 - sig))
    acc[F : 2 * F, :] = gate * sig
    recv("l3", l3_in, to_h)
    logits = (l3_out[...] + l3_in[...]).reshape(H * T8, LANES)

    log_student = log_softmax(logits)
    p_student = jnp.exp(log_student)
    d_own = jnp.where(valid, loss_scale * (2.0 * p_student - onehot - p_teacher), 0.0)
    dl[c, z] = d_own.astype(bf16)
    for k in around:
        pass_on(f"l4_{k}", dl.at[c, z], to_z(k))
    terms = jnp.where(valid, p_teacher * (log_teacher - log_student) - onehot * log_student, 0.0)
    loss = jnp.broadcast_to(jnp.sum(terms, axis=1, keepdims=True), (H * T8, LANES))
    loss_s[...] = loss.reshape(H, T8, LANES)
    loss_rows = jnp.concatenate([loss_s[h], jnp.zeros((LANES - T8, LANES), f32)], axis=0)
    loss_o[...] = loss_rows.T[0:1, 0:T8]
    for k in reversed(around):
        recv(f"l4_{k}", dl.at[c, zat(-k)], to_z(-k))
    pass_on("l5", dl.at[c], to_c)
    recv("l5", dl.at[1 - c], to_c)
    d_logits = jnp.concatenate(
        [dl[k].astype(f32).reshape(Z * H, 1, T8, LANES) for k in range(C)], axis=1
    ).reshape(tokens, LANES)

    d_logits = d_logits.astype(bf16)
    d_units = nt(m_high, d_logits) + nt(m_low, d_logits)
    acc[0:F, :] = d_units * acc[0:F, :]
    acc[F : 2 * F, :] = d_units * acc[F : 2 * F, :]
    d_both = acc[...].astype(bf16)

    ends = {j: ((CUT, CUT_1) if j == 1 else (0, CUT)) for j in range(Y)}

    def partial(dx, j):
        g = gat(dx, j)
        grads[(dx % X) * Y + j] = nn(d_both, normed_columns(g)).astype(bf16)

    def slot(dx, j):
        return (dx % X) * Y + j

    def piece(ref, first, last):
        return ref.at[pl.ds(first, last - first)]

    def early_rs():
        for dx in (2, 1, -1, 0):
            partial(dx, 1)
            send(f"rq{dx % X}", piece(grads.at[slot(dx, 1)], 0, CUT), rq.at[dx % X], to_y(1))

    def take_early(dx):
        recv(f"rq{dx % X}", rq.at[dx % X], to_y(1))
        at = slot(dx, 0)
        grads[at, 0:CUT, :] = (grads[at, 0:CUT, :].astype(f32) + rq[dx % X].astype(f32)).astype(bf16)

    def fill(dx, j):
        if j != 1:
            partial(dx, j)
        if j == 0:
            take_early(dx)

    def start_rs(j):
        first, mid = ends[j]
        fill(2, j)
        opposite = grads.at[slot(2, j)]
        send(f"ra{j}", piece(opposite, first, mid), piece(ra.at[j], 0, mid - first), to_x(1))
        send(f"rb{j}", piece(opposite, mid, 2 * F), piece(rb.at[j], 0, 2 * F - mid), to_x(-1))

    def join_rs(j):
        first, mid = ends[j]
        fill(1, j)
        recv(f"ra{j}", piece(ra.at[j], 0, mid - first), to_x(-1))
        at = slot(1, j)
        joined = grads[at, first:mid, :].astype(f32) + ra[j, 0 : mid - first, :].astype(f32)
        grads[at, first:mid, :] = joined.astype(bf16)
        send(f"sp{j}", piece(grads.at[at], first, 2 * F), piece(sp.at[j], first, 2 * F), to_x(1))
        fill(-1, j)
        recv(f"rb{j}", piece(rb.at[j], 0, 2 * F - mid), to_x(1))
        at = slot(-1, j)
        joined = grads[at, mid : 2 * F, :].astype(f32) + rb[j, 0 : 2 * F - mid, :].astype(f32)
        grads[at, mid : 2 * F, :] = joined.astype(bf16)
        send(f"sm{j}", piece(grads.at[at], first, 2 * F), piece(sm.at[j], first, 2 * F), to_x(-1))
        fill(0, j)

    def finish_rs(j):
        first, mid = ends[j]
        recv(f"sp{j}", piece(sp.at[j], first, 2 * F), to_x(-1))
        recv(f"sm{j}", piece(sm.at[j], first, 2 * F), to_x(1))
        at = slot(0, j)
        rows_j = slice(first, 2 * F)
        total = grads[at, rows_j, :].astype(f32) + sp[j, rows_j, :].astype(f32) + sm[j, rows_j, :].astype(f32)
        if j == 2:
            recv("ry3", ry.at[2], to_y(1))
            total = total + ry[2].astype(f32)
        if j == 0:
            return total
        grads[at, rows_j, :] = total.astype(bf16)
        send(f"ry{j}", piece(grads.at[at], first, 2 * F), piece(ry.at[j - 1], first, 2 * F), to_y(2 if j == 2 else 1))

    start_rs(3)
    early_rs()
    start_rs(2)
    product = nn(units_s[...].astype(bf16), d_logits)
    nred[...] = jnp.concatenate([product, tail], axis=0).reshape(nred.shape)
    sum_start("n", nred, nrx)
    join_rs(3)
    start_rs(1)
    join_rs(2)
    start_rs(0)
    finish_rs(3)
    join_rs(1)
    sum_middle("n", nred, nrx, nry)
    finish_rs(2)
    join_rs(0)
    sum_spread("n", nred, nrx, nry)
    finish_rs(1)
    n_high, n_low = split(sum_end("n", nred, nrx, nry))
    head_block = head_own[...].astype(bf16)
    gd_o[...] = nn(n_high, head_block) + nn(n_low, head_block)
    acc[:, 0:RB] = finish_rs(0)
    recv("ry2", ry.at[1], to_y(2))
    acc[:, 0:RB] += ry[1].astype(f32)
    recv("ry1", piece(ry.at[0], CUT, 2 * F), to_y(1))
    acc[CUT : 2 * F, 0:RB] += ry[0, CUT : 2 * F, :].astype(f32)
    gg_o[...] = acc[0:F, 0:RB]
    gu_o[...] = acc[F : 2 * F, 0:RB]
    wires.finish()


def hand_over(*refs):
    half = len(refs) // 2
    for taken, given in zip(refs[:half], refs[half:]):
        given[...] = taken[...]


def solution(mesh):
    Z = mesh.shape["shard"] // (H * C)
    names = wire_names(Z)

    def local(hidden, norm_gain, gate_codes, gate_scales, up_codes, up_scales, down_codes, down_scales, head, teacher, targets):
        T8, D = hidden.shape
        RB, F = gate_codes.shape
        B = head.shape[1]
        tokens = teacher.shape[0]
        KH = D // 2
        chunk = -(-F // (8 * X)) * 8
        vmem = pl.BlockSpec(memory_space=pltpu.VMEM)
        smem = pl.BlockSpec(memory_space=pltpu.SMEM)
        grad = jax.ShapeDtypeStruct((F, RB), f32)
        V = pltpu.VMEM
        scratch = [
            V((2, T8, KH), f32),
            V((2, T8, KH), f32),
            V((2, Z * H, 2 * T8, KH), bf16),
            V((X * Y, 2 * F, RB), bf16),
            V((128, 256), f32),
            V((LANES, RB), f32),
            V((T8, LANES), f32),
            V((LANES, tokens), f32),
            V((tokens // T8, T8, LANES), f32),
            V((2 * F, tokens), f32),
            V((F, tokens), f32),
            V((X, chunk, LANES), f32),
            V((X, chunk, LANES), f32),
            V((X, chunk, LANES), f32),
            V((X + Y, chunk, LANES), f32),
            V((X, chunk, LANES), f32),
            V((X, chunk, LANES), f32),
            V((X + Y, chunk, LANES), f32),
            V((C, Z, H, T8, LANES), f32),
            V((Z, H, T8, LANES), f32),
            V((Z, H * T8, LANES), bf16),
            V((Z, H * T8, LANES), bf16),
            V((H, T8, LANES), f32),
            V((H, T8, LANES), f32),
            V((C, Z, H * T8, LANES), bf16),
            V((H, T8, LANES), f32),
            V((X * Y, 2 * F, RB), bf16),
            V((Y, CUT, RB), bf16),
            V((Y, 2 * F - CUT, RB), bf16),
            V((Y, 2 * F, RB), bf16),
            V((Y, 2 * F, RB), bf16),
            V((Y - 1, 2 * F, RB), bf16),
            V((X, CUT, RB), bf16),
            pltpu.SemaphoreType.DMA((len(names),)),
            pltpu.SemaphoreType.DMA((len(names),)),
        ]
        loss, gate, up, down = pl.pallas_call(
            functools.partial(kernel, names, Z, D, F, B),
            out_shape=(jax.ShapeDtypeStruct((1, T8), f32), grad, grad, grad),
            in_specs=[pl.BlockSpec()] * 10 + [smem],
            out_specs=(vmem,) * 4,
            scratch_shapes=scratch,
            compiler_params=pltpu.CompilerParams(
                collective_id=0, has_side_effects=True, vmem_limit_bytes=62 << 20
            ),
            name="step",
        )(
            hidden, norm_gain.reshape(1, D), gate_codes.T, gate_scales, up_codes.T, up_scales,
            down_codes.T, down_scales, head.T, teacher.T, targets,
        )
        results = (loss, gate, up, down)
        loss, gate, up, down = pl.pallas_call(
            hand_over,
            out_shape=tuple(jax.ShapeDtypeStruct(r.shape, r.dtype) for r in results),
            in_specs=[pl.BlockSpec()] * 4,
            out_specs=(pl.BlockSpec(),) * 4,
            compiler_params=pltpu.CompilerParams(vmem_limit_bytes=62 << 20),
            name="hand_over",
        )(*results)
        return (loss.reshape(T8), gate.T, up.T, down.T)

    in_specs = (
        P(("grp", "shard"), None),
        P(),
        P("grp", "shard"),
        P("grp", "shard"),
        P("grp", "shard"),
        P("grp", "shard"),
        P("grp", "shard"),
        P("grp", "shard"),
        P(),
        P("grp", None),
        P("grp"),
    )
    out_specs = (P(("grp", "shard")), P("grp", "shard"), P("grp", "shard"), P("grp", "shard"))
    return jax.shard_map(local, mesh=mesh, in_specs=in_specs, out_specs=out_specs, check_vma=False)
```

```python
import functools

import jax
import jax.numpy as jnp
from jax import lax
from jax.experimental import pallas as pl
from jax.experimental.pallas import tpu as pltpu
from jax.sharding import PartitionSpec as P

eps = 1e-05
loss_scale = 64.0
MESH = pl.DeviceIdType.MESH
f32, bf16 = jnp.float32, jnp.bfloat16

X, Y = 4, 4
H, C = 2, 2
REACH = ((0, 1, 1, 1, 1, 1, 1), (0, 1, 1, 1, 1, 1, 0))
CUT = 160
CUT_1 = 240
LANES = 128


def nt(left, right):
    return lax.dot_general(left, right, (((1,), (1,)), ((), ())), preferred_element_type=f32)


def nn(left, right):
    return jnp.dot(left, right, preferred_element_type=f32)


def tn(left, right):
    return lax.dot_general(left, right, (((0,), (0,)), ((), ())), preferred_element_type=f32)


def split(value):
    high = value.astype(bf16)
    return high, (value - high.astype(f32)).astype(bf16)


class Wires:
    def __init__(self, send_sems, recv_sems, names):
        self.send_sems, self.recv_sems, self.names, self.started = send_sems, recv_sems, names, []

    def slot(self, name):
        return self.names[name]

    def describe(self, name, src, dst, device):
        at = self.slot(name)
        return pltpu.make_async_remote_copy(
            src_ref=src,
            dst_ref=dst,
            send_sem=self.send_sems.at[at],
            recv_sem=self.recv_sems.at[at],
            device_id=device,
            device_id_type=MESH,
        )

    def send(self, name, src, dst, device):
        copy = self.describe(name, src, dst, device)
        copy.start()
        self.started.append(copy)

    def recv(self, name, dst, device):
        self.describe(name, dst, dst, device).wait_recv()

    def finish(self):
        for copy in self.started:
            copy.wait_send()


def wire_names(Z):
    half = Z // 2
    names = ["e", "hx0", "hx1", "hy0", "hy1", "l1", "l3", "l5"]
    for j in range(Y):
        names += [f"{kind}{j}" for kind in ("fp", "fm", "ra", "rb", "sp", "sm", "ry", "rq")]
        names += [f"{kind}{p}{j}" for kind in ("y", "xp", "xm") for p in "AB"]
    for s in range(2):
        for n in range(1, half + 1):
            names += [f"z{way}{s}{q}_{n}" for way in "pm" for q in range(2)]
        for k in range(-half, half + 1):
            names.append(f"c{s}_{k}")
    for k in range(1, Z):
        names += [f"l2_{k}", f"l4_{k}"]
    for kind in ("m", "n"):
        for k in range(1, X):
            names += [f"{kind}r{k}", f"{kind}a{k}"]
        for j in range(1, Y):
            names.append(f"{kind}y{j}")
    return {name: at for at, name in enumerate(names)}


def kernel(
    names, Z, D, F, B,
    hid, gain, gc, gs, uc, us, dc, ds, head, teach, targ,
    loss_o, gg_o, gu_o, gd_o,
    halves, pair, nb, wt, scale_pad, head_own, own_logit, teach_pad, teach_rows,
    acc, units_s, whole, mred, mrx, mry, nred, nrx, nry,
    part, l1_in, summed, l2_in, l3_out, l3_in, dl, loss_s,
    grads, ra, rb, sp, sm, ry, rq,
    send_sems, recv_sems,
):
    grp, sh = lax.axis_index("grp"), lax.axis_index("shard")
    x, y = lax.div(grp, Y), lax.rem(grp, Y)
    z, h, c = lax.div(sh, H * C), lax.rem(lax.div(sh, C), H), lax.rem(sh, C)
    half = Z // 2
    RB = D // (X * Y)
    T8 = hid.shape[0]
    KH = D // 2

    def xat(dx):
        return lax.rem(x + dx % X, X) if dx % X else x

    def yat(j):
        return (y, y + 1 - 2 * lax.rem(y, 2), y + 2 - 4 * lax.div(y, 2), 3 - y)[j]

    def zat(dz):
        return lax.rem(z + dz % Z, Z) if dz % Z else z

    def to_x(dx):
        return {"grp": xat(dx) * Y + y}

    def to_y(j):
        return {"grp": x * Y + yat(j)}

    def hat(flip):
        return 1 - h if flip else h

    def to_z(dz, flip=0):
        return {"shard": (zat(dz) * H + hat(flip)) * C + c}

    to_h = to_z(0, 1)
    to_c = {"shard": (z * H + h) * C + (1 - c)}

    wires = Wires(send_sems, recv_sems, names)
    send, recv = wires.send, wires.recv

    barrier = pltpu.get_barrier_semaphore()
    around = sorted(range(1, Z), key=lambda k: -min(k, Z - k))
    peers = [to_z(k) for k in around] + [to_h]
    peers += [to_y(j) for j in range(1, Y)] + [to_x(k) for k in range(1, X)] + [to_c]
    for peer in peers:
        pl.semaphore_signal(barrier, inc=1, device_id=peer, device_id_type=MESH)

    xf = hid[...].astype(f32)
    mean = jnp.mean(xf * xf, axis=1, keepdims=True)
    normed = (xf * lax.rsqrt(mean + eps) * gain[...]).astype(bf16).astype(f32)
    halves[0] = normed[:, :KH]
    halves[1] = normed[:, KH:]
    pair[c] = halves[c]

    pl.semaphore_wait(barrier, len(peers))
    send("e", halves.at[1 - c], pair.at[c], to_c)

    scale_pad[...] = jnp.zeros_like(scale_pad)
    scale_pad[0:2, 0:F] = gs[...]
    scale_pad[8:10, 0:F] = us[...]
    scale_pad[16:18, 0:F] = ds[...]
    columns = scale_pad[...].T

    def dequantize(codes, at):
        value = codes[...].astype(f32)
        mid = RB // 2
        left = value[:, :mid] * columns[:F, at : at + 1]
        right = value[:, mid:] * columns[:F, at + 1 : at + 2]
        return jnp.concatenate([left, right], axis=1)

    wt[grp] = jnp.concatenate([dequantize(gc, 0), dequantize(uc, 8)], axis=0).astype(bf16)

    def gat(dx, j):
        return xat(dx) * Y + yat(j)

    def rows_of(block, p):
        return block.at[pl.ds(0, CUT)] if p == "A" else block.at[pl.ds(CUT, 2 * F - CUT)]

    def pass_on(name, block, device):
        send(name, block, block, device)

    def spread_x(j):
        block = wt.at[gat(0, j)]
        if j:
            recv(f"yA{j}", rows_of(block, "A"), to_y(j))
        if j == 2:
            pass_on("yA3", rows_of(block, "A"), to_y(1))
        pass_on(f"xpA{j}", rows_of(block, "A"), to_x(1))
        if j:
            recv(f"yB{j}", rows_of(block, "B"), to_y(j))
        if j == 2:
            pass_on("yB3", rows_of(block, "B"), to_y(1))
        pass_on(f"xmB{j}", rows_of(block, "B"), to_x(-1))
        pass_on(f"xpB{j}", rows_of(block, "B"), to_x(1))
        pass_on(f"xmA{j}", rows_of(block, "A"), to_x(-1))

    def forward_x(j):
        low, high = rows_of(wt.at[gat(-1, j)], "A"), rows_of(wt.at[gat(1, j)], "B")
        recv(f"xpA{j}", low, to_x(-1))
        pass_on(f"fp{j}", low, to_x(1))
        recv(f"xmB{j}", high, to_x(1))
        pass_on(f"fm{j}", high, to_x(-1))

    def finish_x(j):
        recv(f"xpB{j}", rows_of(wt.at[gat(-1, j)], "B"), to_x(-1))
        recv(f"xmA{j}", rows_of(wt.at[gat(1, j)], "A"), to_x(1))
        opposite = wt.at[gat(2, j)]
        recv(f"fp{j}", rows_of(opposite, "A"), to_x(-1))
        recv(f"fm{j}", rows_of(opposite, "B"), to_x(1))

    def start_y(p, j):
        pass_on(f"y{p}{j}", rows_of(wt.at[grp], p), to_y(j))

    def block_of(s, dz):
        return nb.at[c, zat(dz) * H + (h if s == 0 else 1 - h)]

    def other_block_of(s, dz):
        return nb.at[1 - c, zat(dz) * H + (h if s == 0 else 1 - h)]

    def column_half(ref, at):
        return ref.at[:, pl.ds(at * (KH // 2), KH // 2)]

    def one_way(s, d, q, sign):
        return d < half or (s == 0 and (q == 0) == (sign == 1))

    def next_z(s, d, q):
        for reach in (2, 1):
            for way, sign in (("p", 1), ("m", -1)):
                goal = d + reach
                if goal <= half and REACH[s][goal] == reach and one_way(s, goal, q, sign):
                    block = column_half(block_of(s, -sign * d), q)
                    pass_on(f"z{way}{s}{q}_{goal}", block, to_z(sign * reach))

    def start_z(s):
        for q in range(2):
            if s:
                recv(f"hx{q}", column_half(block_of(s, 0), q), to_h)
            next_z(s, 0, q)
        pass_on(f"c{s}_0", block_of(s, 0), to_c)

    def step_z(s, d):
        for q in range(2):
            block = column_half(block_of(s, half), q)
            if s == 1 and d == half:
                recv(f"hy{q}", block, to_h)
            for way, sign in (("p", 1), ("m", -1)):
                if one_way(s, d, q, sign):
                    recv(f"z{way}{s}{q}_{d}", column_half(block_of(s, -sign * d), q), to_z(-sign * REACH[s][d]))
            if s == 0 and d == half:
                pass_on(f"hy{q}", block, to_h)
            if d < half:
                next_z(s, d, q)
        if d < half:
            pass_on(f"c{s}_{-d}", block_of(s, -d), to_c)
        pass_on(f"c{s}_{d}", block_of(s, d), to_c)

    def sum_start(kind, red, rx):
        for k in range(1, X):
            send(f"{kind}r{k}", red.at[xat(k)], rx.at[k - 1], to_x(k))

    def sum_middle(kind, red, rx, ry_):
        for k in range(1, X):
            recv(f"{kind}r{k}", rx.at[k - 1], to_x(-k))
        ry_[0] = red[x] + rx[0] + rx[1] + rx[2]
        for j in range(1, Y):
            send(f"{kind}y{j}", ry_.at[0], ry_.at[j], to_y(j))

    def sum_spread(kind, red, rx, ry_):
        for j in range(1, Y):
            recv(f"{kind}y{j}", ry_.at[j], to_y(j))
        rx[X - 1] = ry_[0] + ry_[1] + ry_[2] + ry_[3]
        for k in range(1, X):
            send(f"{kind}a{k}", rx.at[X - 1], ry_.at[Y + k - 1], to_x(k))

    def sum_end(kind, red, rx, ry_):
        whole[x] = rx[X - 1]
        for k in range(1, X):
            recv(f"{kind}a{k}", ry_.at[Y + k - 1], to_x(-k))
            whole[xat(-k)] = ry_[Y + k - 1]
        return whole[...].reshape(red.shape[0] * red.shape[1], LANES)[:F]

    recv("e", pair.at[1 - c], to_c)
    nb[c, z * H + h] = pair[...].reshape(2 * T8, KH).astype(bf16)
    own = block_of(0, 0)
    for q in range(2):
        pass_on(f"hx{q}", column_half(own, q), to_h)
    start_z(0)
    spread_x(0)
    for j in (1, 2):
        for p in "AB":
            start_y(p, j)

    head_own[...] = jnp.zeros_like(head_own)
    head_own[0:B, :] = head[:, pl.ds(pl.multiple_of(grp * RB, RB), RB)].astype(f32)
    head_block = head_own[...].astype(bf16)
    w_down = dequantize(dc, 16).astype(bf16)
    product = nt(w_down, head_block)
    rows = mred.shape[0] * mred.shape[1]
    tail = jnp.zeros((rows - F, LANES), f32)
    mred[...] = jnp.concatenate([product, tail], axis=0).reshape(mred.shape)
    sum_start("m", mred, mrx)

    step_z(0, 1)
    forward_x(0)
    step_z(0, 2)
    start_z(1)
    spread_x(1)
    step_z(0, 3)
    step_z(1, 1)
    spread_x(2)
    step_z(0, 4)
    step_z(1, 2)
    forward_x(1)
    step_z(0, 5)
    step_z(1, 3)
    spread_x(3)
    forward_x(2)
    sum_middle("m", mred, mrx, mry)
    step_z(0, 6)
    step_z(1, 4)
    forward_x(3)
    sum_spread("m", mred, mrx, mry)
    step_z(1, 5)
    step_z(1, 6)
    for j in range(Y):
        finish_x(j)
    m_high, m_low = split(sum_end("m", mred, mrx, mry))
    for s in range(2):
        for k in range(-half + 1, half + 1):
            recv(f"c{s}_{k}", other_block_of(s, k), to_c)

    tokens = acc.shape[1]
    per = X * Y // 2

    def normed_columns(g):
        at = lax.rem(g, per)
        return nb[lax.div(g, per), :, :, pl.ds(pl.multiple_of(at * RB, RB), RB)].reshape(tokens, RB)

    total = nt(wt[0], normed_columns(0))
    for g in range(1, X * Y):
        total = total + nt(wt[g], normed_columns(g))
    acc[...] = total
    gate, up = acc[0:F, :], acc[F : 2 * F, :]
    sig = jax.nn.sigmoid(gate)
    units = (gate * sig * up).astype(bf16)
    units_s[...] = units.astype(f32)

    share = tn(units, jnp.concatenate([m_high, m_low], axis=1))
    share = (share[:, :LANES] + share[:, LANES:]).reshape(Z * H, C, T8, LANES)
    part[0] = share[:, 0].reshape(Z, H, T8, LANES)
    part[1] = share[:, 1].reshape(Z, H, T8, LANES)
    send("l1", part.at[1 - c], l1_in, to_c)
    recv("l1", l1_in, to_c)
    shares = part[c] + l1_in[...]
    summed[...] = shares.reshape(Z, H * T8, LANES).astype(bf16)
    for k in around:
        send(f"l2_{k}", summed.at[zat(k)], l2_in.at[k], to_z(k))

    own_logit[...] = jnp.zeros_like(own_logit)
    own_logit[:, 0:B] = nt(hid[...], head[...])
    teach_pad[...] = jnp.zeros_like(teach_pad)
    teach_pad[0:B, :] = teach[...]
    teach_rows[...] = teach_pad[...].T.reshape(teach_rows.shape)
    lane = lax.broadcasted_iota(jnp.int32, (H * T8, LANES), 1)
    sub = lax.broadcasted_iota(jnp.int32, (H * T8, LANES), 0)
    valid = lane < B
    first = (z * H * C + c) * T8
    wanted = jnp.zeros((H * T8, LANES), jnp.int32)
    for at in range(H * T8):
        value = targ[first + (at // T8) * C * T8 + at % T8]
        wanted = jnp.where(sub == at, value, wanted)
    onehot = jnp.where(lane == wanted, 1.0, 0.0)

    def log_softmax(values):
        top = jnp.max(jnp.where(valid, values, -jnp.inf), axis=1, keepdims=True)
        shifted = jnp.where(valid, values - top, 0.0)
        bottom = jnp.sum(jnp.where(valid, jnp.exp(shifted), 0.0), axis=1, keepdims=True)
        return shifted - jnp.log(bottom)

    teacher = jnp.concatenate([teach_rows[z * H * C + k * C + c] for k in range(H)], axis=0)
    log_teacher = log_softmax(teacher)
    p_teacher = jnp.exp(log_teacher)

    total = summed[z].astype(f32)
    for k in reversed(around):
        recv(f"l2_{k}", l2_in.at[k], to_z(-k))
        total = total + l2_in[k].astype(f32)
    l3_out[...] = total.reshape(H, T8, LANES)
    l3_out[h] = l3_out[h] + own_logit[...]
    send("l3", l3_out, l3_in, to_h)
    acc[0:F, :] = up * sig * (1.0 + gate * (1.0 - sig))
    acc[F : 2 * F, :] = gate * sig
    recv("l3", l3_in, to_h)
    logits = (l3_out[...] + l3_in[...]).reshape(H * T8, LANES)

    log_student = log_softmax(logits)
    p_student = jnp.exp(log_student)
    d_own = jnp.where(valid, loss_scale * (2.0 * p_student - onehot - p_teacher), 0.0)
    dl[c, z] = d_own.astype(bf16)
    for k in around:
        pass_on(f"l4_{k}", dl.at[c, z], to_z(k))
    terms = jnp.where(valid, p_teacher * (log_teacher - log_student) - onehot * log_student, 0.0)
    loss = jnp.broadcast_to(jnp.sum(terms, axis=1, keepdims=True), (H * T8, LANES))
    loss_s[...] = loss.reshape(H, T8, LANES)
    loss_rows = jnp.concatenate([loss_s[h], jnp.zeros((LANES - T8, LANES), f32)], axis=0)
    loss_o[...] = loss_rows.T[0:1, 0:T8]
    for k in reversed(around):
        recv(f"l4_{k}", dl.at[c, zat(-k)], to_z(-k))
    pass_on("l5", dl.at[c], to_c)
    recv("l5", dl.at[1 - c], to_c)
    d_logits = jnp.concatenate(
        [dl[k].astype(f32).reshape(Z * H, 1, T8, LANES) for k in range(C)], axis=1
    ).reshape(tokens, LANES)

    d_logits = d_logits.astype(bf16)
    d_units = nt(jnp.concatenate([m_high.astype(f32), m_low.astype(f32)], axis=0).astype(bf16), d_logits)
    d_units = d_units[0:F] + d_units[F : 2 * F]
    acc[0:F, :] = d_units * acc[0:F, :]
    acc[F : 2 * F, :] = d_units * acc[F : 2 * F, :]
    d_both = acc[...].astype(bf16)

    ends = {j: ((CUT, CUT_1) if j == 1 else (0, CUT)) for j in range(Y)}

    def partial(dx, j):
        g = gat(dx, j)
        grads[(dx % X) * Y + j] = nn(d_both, normed_columns(g)).astype(bf16)

    def slot(dx, j):
        return (dx % X) * Y + j

    def piece(ref, first, last):
        return ref.at[pl.ds(first, last - first)]

    def early_rs():
        for dx in (2, 1, -1, 0):
            partial(dx, 1)
            send(f"rq{dx % X}", piece(grads.at[slot(dx, 1)], 0, CUT), rq.at[dx % X], to_y(1))

    def take_early(dx):
        recv(f"rq{dx % X}", rq.at[dx % X], to_y(1))
        at = slot(dx, 0)
        grads[at, 0:CUT, :] = (grads[at, 0:CUT, :].astype(f32) + rq[dx % X].astype(f32)).astype(bf16)

    def fill(dx, j):
        if j != 1:
            partial(dx, j)
        if j == 0:
            take_early(dx)

    def start_rs(j):
        first, mid = ends[j]
        fill(2, j)
        opposite = grads.at[slot(2, j)]
        send(f"ra{j}", piece(opposite, first, mid), piece(ra.at[j], 0, mid - first), to_x(1))
        send(f"rb{j}", piece(opposite, mid, 2 * F), piece(rb.at[j], 0, 2 * F - mid), to_x(-1))

    def join_rs(j):
        first, mid = ends[j]
        fill(1, j)
        recv(f"ra{j}", piece(ra.at[j], 0, mid - first), to_x(-1))
        at = slot(1, j)
        joined = grads[at, first:mid, :].astype(f32) + ra[j, 0 : mid - first, :].astype(f32)
        grads[at, first:mid, :] = joined.astype(bf16)
        send(f"sp{j}", piece(grads.at[at], first, 2 * F), piece(sp.at[j], first, 2 * F), to_x(1))
        fill(-1, j)
        recv(f"rb{j}", piece(rb.at[j], 0, 2 * F - mid), to_x(1))
        at = slot(-1, j)
        joined = grads[at, mid : 2 * F, :].astype(f32) + rb[j, 0 : 2 * F - mid, :].astype(f32)
        grads[at, mid : 2 * F, :] = joined.astype(bf16)
        send(f"sm{j}", piece(grads.at[at], first, 2 * F), piece(sm.at[j], first, 2 * F), to_x(-1))
        fill(0, j)

    def finish_rs(j):
        first, mid = ends[j]
        recv(f"sp{j}", piece(sp.at[j], first, 2 * F), to_x(-1))
        recv(f"sm{j}", piece(sm.at[j], first, 2 * F), to_x(1))
        at = slot(0, j)
        rows_j = slice(first, 2 * F)
        total = grads[at, rows_j, :].astype(f32) + sp[j, rows_j, :].astype(f32) + sm[j, rows_j, :].astype(f32)
        if j == 2:
            recv("ry3", ry.at[2], to_y(1))
            total = total + ry[2].astype(f32)
        if j == 0:
            return total
        grads[at, rows_j, :] = total.astype(bf16)
        send(f"ry{j}", piece(grads.at[at], first, 2 * F), piece(ry.at[j - 1], first, 2 * F), to_y(2 if j == 2 else 1))

    start_rs(3)
    early_rs()
    start_rs(2)
    product = nn(units_s[...].astype(bf16), d_logits)
    nred[...] = jnp.concatenate([product, tail], axis=0).reshape(nred.shape)
    sum_start("n", nred, nrx)
    join_rs(3)
    start_rs(1)
    join_rs(2)
    start_rs(0)
    finish_rs(3)
    join_rs(1)
    sum_middle("n", nred, nrx, nry)
    finish_rs(2)
    join_rs(0)
    sum_spread("n", nred, nrx, nry)
    finish_rs(1)
    n_high, n_low = split(sum_end("n", nred, nrx, nry))
    head_block = head_own[...].astype(bf16)
    gd_o[...] = nn(n_high, head_block) + nn(n_low, head_block)
    acc[:, 0:RB] = finish_rs(0)
    recv("ry2", ry.at[1], to_y(2))
    acc[:, 0:RB] += ry[1].astype(f32)
    recv("ry1", piece(ry.at[0], CUT, 2 * F), to_y(1))
    acc[CUT : 2 * F, 0:RB] += ry[0, CUT : 2 * F, :].astype(f32)
    gg_o[...] = acc[0:F, 0:RB]
    gu_o[...] = acc[F : 2 * F, 0:RB]
    wires.finish()


def hand_over(*refs):
    half = len(refs) // 2
    for taken, given in zip(refs[:half], refs[half:]):
        given[...] = taken[...]


def solution(mesh):
    Z = mesh.shape["shard"] // (H * C)
    names = wire_names(Z)

    def local(hidden, norm_gain, gate_codes, gate_scales, up_codes, up_scales, down_codes, down_scales, head, teacher, targets):
        T8, D = hidden.shape
        RB, F = gate_codes.shape
        B = head.shape[1]
        tokens = teacher.shape[0]
        KH = D // 2
        chunk = -(-F // (8 * X)) * 8
        vmem = pl.BlockSpec(memory_space=pltpu.VMEM)
        smem = pl.BlockSpec(memory_space=pltpu.SMEM)
        grad = jax.ShapeDtypeStruct((F, RB), f32)
        V = pltpu.VMEM
        scratch = [
            V((2, T8, KH), f32),
            V((2, T8, KH), f32),
            V((2, Z * H, 2 * T8, KH), bf16),
            V((X * Y, 2 * F, RB), bf16),
            V((128, 256), f32),
            V((LANES, RB), f32),
            V((T8, LANES), f32),
            V((LANES, tokens), f32),
            V((tokens // T8, T8, LANES), f32),
            V((2 * F, tokens), f32),
            V((F, tokens), f32),
            V((X, chunk, LANES), f32),
            V((X, chunk, LANES), f32),
            V((X, chunk, LANES), f32),
            V((X + Y, chunk, LANES), f32),
            V((X, chunk, LANES), f32),
            V((X, chunk, LANES), f32),
            V((X + Y, chunk, LANES), f32),
            V((C, Z, H, T8, LANES), f32),
            V((Z, H, T8, LANES), f32),
            V((Z, H * T8, LANES), bf16),
            V((Z, H * T8, LANES), bf16),
            V((H, T8, LANES), f32),
            V((H, T8, LANES), f32),
            V((C, Z, H * T8, LANES), bf16),
            V((H, T8, LANES), f32),
            V((X * Y, 2 * F, RB), bf16),
            V((Y, CUT, RB), bf16),
            V((Y, 2 * F - CUT, RB), bf16),
            V((Y, 2 * F, RB), bf16),
            V((Y, 2 * F, RB), bf16),
            V((Y - 1, 2 * F, RB), bf16),
            V((X, CUT, RB), bf16),
            pltpu.SemaphoreType.DMA((len(names),)),
            pltpu.SemaphoreType.DMA((len(names),)),
        ]
        loss, gate, up, down = pl.pallas_call(
            functools.partial(kernel, names, Z, D, F, B),
            out_shape=(jax.ShapeDtypeStruct((1, T8), f32), grad, grad, grad),
            in_specs=[pl.BlockSpec()] * 10 + [smem],
            out_specs=(vmem,) * 4,
            scratch_shapes=scratch,
            compiler_params=pltpu.CompilerParams(
                collective_id=0, has_side_effects=True, vmem_limit_bytes=62 << 20
            ),
            name="step",
        )(
            hidden, norm_gain.reshape(1, D), gate_codes.T, gate_scales, up_codes.T, up_scales,
            down_codes.T, down_scales, head.T, teacher.T, targets,
        )
        results = (loss, gate, up, down)
        loss, gate, up, down = pl.pallas_call(
            hand_over,
            out_shape=tuple(jax.ShapeDtypeStruct(r.shape, r.dtype) for r in results),
            in_specs=[pl.BlockSpec()] * 4,
            out_specs=(pl.BlockSpec(),) * 4,
            compiler_params=pltpu.CompilerParams(vmem_limit_bytes=62 << 20),
            name="hand_over",
        )(*results)
        return (loss.reshape(T8), gate.T, up.T, down.T)

    in_specs = (
        P(("grp", "shard"), None),
        P(),
        P("grp", "shard"),
        P("grp", "shard"),
        P("grp", "shard"),
        P("grp", "shard"),
        P("grp", "shard"),
        P("grp", "shard"),
        P(),
        P("grp", None),
        P("grp"),
    )
    out_specs = (P(("grp", "shard")), P("grp", "shard"), P("grp", "shard"), P("grp", "shard"))
    return jax.shard_map(local, mesh=mesh, in_specs=in_specs, out_specs=out_specs, check_vma=False)
```

```python
import functools

import jax
import jax.numpy as jnp
from jax import lax
from jax.experimental import pallas as pl
from jax.experimental.pallas import tpu as pltpu
from jax.sharding import PartitionSpec as P

eps = 1e-05
loss_scale = 64.0
MESH = pl.DeviceIdType.MESH
f32, bf16 = jnp.float32, jnp.bfloat16

X, Y = 4, 4
H, C = 2, 2
REACH = ((0, 1, 1, 1, 1, 1, 1), (0, 1, 1, 1, 1, 1, 0))
CUT = 160
CUT_1 = 240
LANES = 128


def nt(left, right):
    return lax.dot_general(left, right, (((1,), (1,)), ((), ())), preferred_element_type=f32)


def nn(left, right):
    return jnp.dot(left, right, preferred_element_type=f32)


def tn(left, right):
    return lax.dot_general(left, right, (((0,), (0,)), ((), ())), preferred_element_type=f32)


def split(value):
    high = value.astype(bf16)
    return high, (value - high.astype(f32)).astype(bf16)


class Wires:
    def __init__(self, send_sems, recv_sems, names):
        self.send_sems, self.recv_sems, self.names, self.started = send_sems, recv_sems, names, []

    def slot(self, name):
        return self.names[name]

    def describe(self, name, src, dst, device):
        at = self.slot(name)
        return pltpu.make_async_remote_copy(
            src_ref=src,
            dst_ref=dst,
            send_sem=self.send_sems.at[at],
            recv_sem=self.recv_sems.at[at],
            device_id=device,
            device_id_type=MESH,
        )

    def send(self, name, src, dst, device):
        copy = self.describe(name, src, dst, device)
        copy.start()
        self.started.append(copy)

    def recv(self, name, dst, device):
        self.describe(name, dst, dst, device).wait_recv()

    def finish(self):
        for copy in self.started:
            copy.wait_send()


def wire_names(Z):
    half = Z // 2
    names = ["e", "hx0", "hx1", "hy0", "hy1", "l1", "l3", "l5"]
    for j in range(Y):
        names += [f"{kind}{j}" for kind in ("fp", "fm", "ra", "rb", "sp", "sm", "ry", "rq")]
        names += [f"{kind}{p}{j}" for kind in ("y", "xp", "xm") for p in "AB"]
    for s in range(2):
        for n in range(1, half + 1):
            names += [f"z{way}{s}{q}_{n}" for way in "pm" for q in range(2)]
        for k in range(-half, half + 1):
            names.append(f"c{s}_{k}")
    for k in range(1, Z):
        names += [f"l2_{k}", f"l4_{k}"]
    for kind in ("m", "n"):
        for k in range(1, X):
            names += [f"{kind}r{k}", f"{kind}a{k}"]
        for j in range(1, Y):
            names.append(f"{kind}y{j}")
    return {name: at for at, name in enumerate(names)}


def kernel(
    names, Z, D, F, B,
    hid, gain, gc, gs, uc, us, dc, ds, head, teach, targ,
    loss_o, gg_o, gu_o, gd_o,
    halves, pair, nb, wt, scale_pad, head_own, own_logit, teach_pad, teach_rows,
    acc, units_s, whole, mred, mrx, mry, nred, nrx, nry,
    part, l1_in, summed, l2_in, l3_out, l3_in, dl, loss_s,
    grads, ra, rb, sp, sm, ry, rq,
    send_sems, recv_sems,
):
    grp, sh = lax.axis_index("grp"), lax.axis_index("shard")
    x, y = lax.div(grp, Y), lax.rem(grp, Y)
    z, h, c = lax.div(sh, H * C), lax.rem(lax.div(sh, C), H), lax.rem(sh, C)
    half = Z // 2
    RB = D // (X * Y)
    T8 = hid.shape[0]
    KH = D // 2

    def xat(dx):
        return lax.rem(x + dx % X, X) if dx % X else x

    def yat(j):
        return (y, y + 1 - 2 * lax.rem(y, 2), y + 2 - 4 * lax.div(y, 2), 3 - y)[j]

    def zat(dz):
        return lax.rem(z + dz % Z, Z) if dz % Z else z

    def to_x(dx):
        return {"grp": xat(dx) * Y + y}

    def to_y(j):
        return {"grp": x * Y + yat(j)}

    def hat(flip):
        return 1 - h if flip else h

    def to_z(dz, flip=0):
        return {"shard": (zat(dz) * H + hat(flip)) * C + c}

    to_h = to_z(0, 1)
    to_c = {"shard": (z * H + h) * C + (1 - c)}

    wires = Wires(send_sems, recv_sems, names)
    send, recv = wires.send, wires.recv

    barrier = pltpu.get_barrier_semaphore()
    around = sorted(range(1, Z), key=lambda k: -min(k, Z - k))
    peers = [to_z(k) for k in around] + [to_h]
    peers += [to_y(j) for j in range(1, Y)] + [to_x(k) for k in range(1, X)] + [to_c]
    for peer in peers:
        pl.semaphore_signal(barrier, inc=1, device_id=peer, device_id_type=MESH)

    xf = hid[...].astype(f32)
    mean = jnp.mean(xf * xf, axis=1, keepdims=True)
    normed = (xf * lax.rsqrt(mean + eps) * gain[...]).astype(bf16).astype(f32)
    halves[0] = normed[:, :KH]
    halves[1] = normed[:, KH:]
    pair[c] = halves[c]

    pl.semaphore_wait(barrier, len(peers))
    send("e", halves.at[1 - c], pair.at[c], to_c)

    scale_pad[...] = jnp.zeros_like(scale_pad)
    scale_pad[0:2, 0:F] = gs[...]
    scale_pad[8:10, 0:F] = us[...]
    scale_pad[16:18, 0:F] = ds[...]
    columns = scale_pad[...].T

    def dequantize(codes, at):
        value = codes[...].astype(f32)
        mid = RB // 2
        left = value[:, :mid] * columns[:F, at : at + 1]
        right = value[:, mid:] * columns[:F, at + 1 : at + 2]
        return jnp.concatenate([left, right], axis=1)

    wt[grp] = jnp.concatenate([dequantize(gc, 0), dequantize(uc, 8)], axis=0).astype(bf16)

    def gat(dx, j):
        return xat(dx) * Y + yat(j)

    def rows_of(block, p):
        return block.at[pl.ds(0, CUT)] if p == "A" else block.at[pl.ds(CUT, 2 * F - CUT)]

    def pass_on(name, block, device):
        send(name, block, block, device)

    def spread_x(j):
        block = wt.at[gat(0, j)]
        if j:
            recv(f"yA{j}", rows_of(block, "A"), to_y(j))
        if j == 2:
            pass_on("yA3", rows_of(block, "A"), to_y(1))
        pass_on(f"xpA{j}", rows_of(block, "A"), to_x(1))
        if j:
            recv(f"yB{j}", rows_of(block, "B"), to_y(j))
        if j == 2:
            pass_on("yB3", rows_of(block, "B"), to_y(1))
        pass_on(f"xmB{j}", rows_of(block, "B"), to_x(-1))
        pass_on(f"xpB{j}", rows_of(block, "B"), to_x(1))
        pass_on(f"xmA{j}", rows_of(block, "A"), to_x(-1))

    def forward_x(j):
        low, high = rows_of(wt.at[gat(-1, j)], "A"), rows_of(wt.at[gat(1, j)], "B")
        recv(f"xpA{j}", low, to_x(-1))
        pass_on(f"fp{j}", low, to_x(1))
        recv(f"xmB{j}", high, to_x(1))
        pass_on(f"fm{j}", high, to_x(-1))

    def finish_x(j):
        recv(f"xpB{j}", rows_of(wt.at[gat(-1, j)], "B"), to_x(-1))
        recv(f"xmA{j}", rows_of(wt.at[gat(1, j)], "A"), to_x(1))
        opposite = wt.at[gat(2, j)]
        recv(f"fp{j}", rows_of(opposite, "A"), to_x(-1))
        recv(f"fm{j}", rows_of(opposite, "B"), to_x(1))

    def start_y(p, j):
        pass_on(f"y{p}{j}", rows_of(wt.at[grp], p), to_y(j))

    def block_of(s, dz):
        return nb.at[c, zat(dz) * H + (h if s == 0 else 1 - h)]

    def other_block_of(s, dz):
        return nb.at[1 - c, zat(dz) * H + (h if s == 0 else 1 - h)]

    def column_half(ref, at):
        return ref.at[:, pl.ds(at * (KH // 2), KH // 2)]

    def one_way(s, d, q, sign):
        return d < half or (s == 0 and (q == 0) == (sign == 1))

    def next_z(s, d, q):
        for reach in (2, 1):
            for way, sign in (("p", 1), ("m", -1)):
                goal = d + reach
                if goal <= half and REACH[s][goal] == reach and one_way(s, goal, q, sign):
                    block = column_half(block_of(s, -sign * d), q)
                    pass_on(f"z{way}{s}{q}_{goal}", block, to_z(sign * reach))

    def start_z(s):
        for q in range(2):
            if s:
                recv(f"hx{q}", column_half(block_of(s, 0), q), to_h)
            next_z(s, 0, q)
        pass_on(f"c{s}_0", block_of(s, 0), to_c)

    def step_z(s, d):
        for q in range(2):
            block = column_half(block_of(s, half), q)
            if s == 1 and d == half:
                recv(f"hy{q}", block, to_h)
            for way, sign in (("p", 1), ("m", -1)):
                if one_way(s, d, q, sign):
                    recv(f"z{way}{s}{q}_{d}", column_half(block_of(s, -sign * d), q), to_z(-sign * REACH[s][d]))
            if s == 0 and d == half:
                pass_on(f"hy{q}", block, to_h)
            if d < half:
                next_z(s, d, q)
        if d < half:
            pass_on(f"c{s}_{-d}", block_of(s, -d), to_c)
        pass_on(f"c{s}_{d}", block_of(s, d), to_c)

    def sum_start(kind, red, rx):
        for k in range(1, X):
            send(f"{kind}r{k}", red.at[xat(k)], rx.at[k - 1], to_x(k))

    def sum_middle(kind, red, rx, ry_):
        for k in range(1, X):
            recv(f"{kind}r{k}", rx.at[k - 1], to_x(-k))
        ry_[0] = red[x] + rx[0] + rx[1] + rx[2]
        for j in range(1, Y):
            send(f"{kind}y{j}", ry_.at[0], ry_.at[j], to_y(j))

    def sum_spread(kind, red, rx, ry_):
        for j in range(1, Y):
            recv(f"{kind}y{j}", ry_.at[j], to_y(j))
        rx[X - 1] = ry_[0] + ry_[1] + ry_[2] + ry_[3]
        for k in range(1, X):
            send(f"{kind}a{k}", rx.at[X - 1], ry_.at[Y + k - 1], to_x(k))

    def sum_end(kind, red, rx, ry_):
        whole[x] = rx[X - 1]
        for k in range(1, X):
            recv(f"{kind}a{k}", ry_.at[Y + k - 1], to_x(-k))
            whole[xat(-k)] = ry_[Y + k - 1]
        return whole[...].reshape(red.shape[0] * red.shape[1], LANES)[:F]

    recv("e", pair.at[1 - c], to_c)
    nb[c, z * H + h] = pair[...].reshape(2 * T8, KH).astype(bf16)
    own = block_of(0, 0)
    for q in range(2):
        pass_on(f"hx{q}", column_half(own, q), to_h)
    start_z(0)
    spread_x(0)
    for j in (1, 2):
        for p in "AB":
            start_y(p, j)

    head_own[...] = jnp.zeros_like(head_own)
    head_own[0:B, :] = head[:, pl.ds(pl.multiple_of(grp * RB, RB), RB)].astype(f32)
    head_block = head_own[...].astype(bf16)
    w_down = dequantize(dc, 16).astype(bf16)
    product = nt(w_down, head_block)
    rows = mred.shape[0] * mred.shape[1]
    tail = jnp.zeros((rows - F, LANES), f32)
    mred[...] = jnp.concatenate([product, tail], axis=0).reshape(mred.shape)
    sum_start("m", mred, mrx)

    step_z(0, 1)
    forward_x(0)
    step_z(0, 2)
    start_z(1)
    spread_x(1)
    step_z(0, 3)
    step_z(1, 1)
    spread_x(2)
    step_z(0, 4)
    step_z(1, 2)
    forward_x(1)
    step_z(0, 5)
    step_z(1, 3)
    spread_x(3)
    forward_x(2)
    sum_middle("m", mred, mrx, mry)
    step_z(0, 6)
    step_z(1, 4)
    forward_x(3)
    sum_spread("m", mred, mrx, mry)
    step_z(1, 5)
    step_z(1, 6)
    for j in range(Y):
        finish_x(j)
    m_high, m_low = split(sum_end("m", mred, mrx, mry))

    tokens = acc.shape[1]
    per = X * Y // 2

    def normed_columns(g):
        at = lax.rem(g, per)
        return nb[lax.div(g, per), :, :, pl.ds(pl.multiple_of(at * RB, RB), RB)].reshape(tokens, RB)

    def add_half(side):
        total = nt(wt[side * per], normed_columns(side * per))
        for k in range(1, per):
            total = total + nt(wt[side * per + k], normed_columns(side * per + k))
        return total

    acc[...] = add_half(c)
    for s in range(2):
        for k in range(-half + 1, half + 1):
            recv(f"c{s}_{k}", other_block_of(s, k), to_c)
    acc[...] += add_half(1 - c)
    gate, up = acc[0:F, :], acc[F : 2 * F, :]
    sig = jax.nn.sigmoid(gate)
    units = (gate * sig * up).astype(bf16)
    units_s[...] = units.astype(f32)

    share = tn(units, jnp.concatenate([m_high, m_low], axis=1))
    share = (share[:, :LANES] + share[:, LANES:]).reshape(Z * H, C, T8, LANES)
    part[0] = share[:, 0].reshape(Z, H, T8, LANES)
    part[1] = share[:, 1].reshape(Z, H, T8, LANES)
    send("l1", part.at[1 - c], l1_in, to_c)
    recv("l1", l1_in, to_c)
    shares = part[c] + l1_in[...]
    summed[...] = shares.reshape(Z, H * T8, LANES).astype(bf16)
    for k in around:
        send(f"l2_{k}", summed.at[zat(k)], l2_in.at[k], to_z(k))

    own_logit[...] = jnp.zeros_like(own_logit)
    own_logit[:, 0:B] = nt(hid[...], head[...])
    teach_pad[...] = jnp.zeros_like(teach_pad)
    teach_pad[0:B, :] = teach[...]
    teach_rows[...] = teach_pad[...].T.reshape(teach_rows.shape)
    lane = lax.broadcasted_iota(jnp.int32, (H * T8, LANES), 1)
    sub = lax.broadcasted_iota(jnp.int32, (H * T8, LANES), 0)
    valid = lane < B
    first = (z * H * C + c) * T8
    wanted = jnp.zeros((H * T8, LANES), jnp.int32)
    for at in range(H * T8):
        value = targ[first + (at // T8) * C * T8 + at % T8]
        wanted = jnp.where(sub == at, value, wanted)
    onehot = jnp.where(lane == wanted, 1.0, 0.0)

    def log_softmax(values):
        top = jnp.max(jnp.where(valid, values, -jnp.inf), axis=1, keepdims=True)
        shifted = jnp.where(valid, values - top, 0.0)
        bottom = jnp.sum(jnp.where(valid, jnp.exp(shifted), 0.0), axis=1, keepdims=True)
        return shifted - jnp.log(bottom)

    teacher = jnp.concatenate([teach_rows[z * H * C + k * C + c] for k in range(H)], axis=0)
    log_teacher = log_softmax(teacher)
    p_teacher = jnp.exp(log_teacher)

    total = summed[z].astype(f32)
    for k in reversed(around):
        recv(f"l2_{k}", l2_in.at[k], to_z(-k))
        total = total + l2_in[k].astype(f32)
    l3_out[...] = total.reshape(H, T8, LANES)
    l3_out[h] = l3_out[h] + own_logit[...]
    send("l3", l3_out, l3_in, to_h)
    acc[0:F, :] = up * sig * (1.0 + gate * (1.0 - sig))
    acc[F : 2 * F, :] = gate * sig
    recv("l3", l3_in, to_h)
    logits = (l3_out[...] + l3_in[...]).reshape(H * T8, LANES)

    log_student = log_softmax(logits)
    p_student = jnp.exp(log_student)
    d_own = jnp.where(valid, loss_scale * (2.0 * p_student - onehot - p_teacher), 0.0)
    dl[c, z] = d_own.astype(bf16)
    for k in around:
        pass_on(f"l4_{k}", dl.at[c, z], to_z(k))
    terms = jnp.where(valid, p_teacher * (log_teacher - log_student) - onehot * log_student, 0.0)
    loss = jnp.broadcast_to(jnp.sum(terms, axis=1, keepdims=True), (H * T8, LANES))
    loss_s[...] = loss.reshape(H, T8, LANES)
    loss_rows = jnp.concatenate([loss_s[h], jnp.zeros((LANES - T8, LANES), f32)], axis=0)
    loss_o[...] = loss_rows.T[0:1, 0:T8]
    for k in reversed(around):
        recv(f"l4_{k}", dl.at[c, zat(-k)], to_z(-k))
    pass_on("l5", dl.at[c], to_c)
    recv("l5", dl.at[1 - c], to_c)
    d_logits = jnp.concatenate(
        [dl[k].astype(f32).reshape(Z * H, 1, T8, LANES) for k in range(C)], axis=1
    ).reshape(tokens, LANES)

    d_logits = d_logits.astype(bf16)
    d_units = nt(jnp.concatenate([m_high.astype(f32), m_low.astype(f32)], axis=0).astype(bf16), d_logits)
    d_units = d_units[0:F] + d_units[F : 2 * F]
    acc[0:F, :] = d_units * acc[0:F, :]
    acc[F : 2 * F, :] = d_units * acc[F : 2 * F, :]
    d_both = acc[...].astype(bf16)

    ends = {j: ((CUT, CUT_1) if j == 1 else (0, CUT)) for j in range(Y)}

    def partial(dx, j):
        g = gat(dx, j)
        grads[(dx % X) * Y + j] = nn(d_both, normed_columns(g)).astype(bf16)

    def slot(dx, j):
        return (dx % X) * Y + j

    def piece(ref, first, last):
        return ref.at[pl.ds(first, last - first)]

    def early_rs():
        for dx in (2, 1, -1, 0):
            partial(dx, 1)
            send(f"rq{dx % X}", piece(grads.at[slot(dx, 1)], 0, CUT), rq.at[dx % X], to_y(1))

    def take_early(dx):
        recv(f"rq{dx % X}", rq.at[dx % X], to_y(1))
        at = slot(dx, 0)
        grads[at, 0:CUT, :] = (grads[at, 0:CUT, :].astype(f32) + rq[dx % X].astype(f32)).astype(bf16)

    def fill(dx, j):
        if j != 1:
            partial(dx, j)
        if j == 0:
            take_early(dx)

    def start_rs(j):
        first, mid = ends[j]
        fill(2, j)
        opposite = grads.at[slot(2, j)]
        send(f"ra{j}", piece(opposite, first, mid), piece(ra.at[j], 0, mid - first), to_x(1))
        send(f"rb{j}", piece(opposite, mid, 2 * F), piece(rb.at[j], 0, 2 * F - mid), to_x(-1))

    def join_rs(j):
        first, mid = ends[j]
        fill(1, j)
        recv(f"ra{j}", piece(ra.at[j], 0, mid - first), to_x(-1))
        at = slot(1, j)
        joined = grads[at, first:mid, :].astype(f32) + ra[j, 0 : mid - first, :].astype(f32)
        grads[at, first:mid, :] = joined.astype(bf16)
        send(f"sp{j}", piece(grads.at[at], first, 2 * F), piece(sp.at[j], first, 2 * F), to_x(1))
        fill(-1, j)
        recv(f"rb{j}", piece(rb.at[j], 0, 2 * F - mid), to_x(1))
        at = slot(-1, j)
        joined = grads[at, mid : 2 * F, :].astype(f32) + rb[j, 0 : 2 * F - mid, :].astype(f32)
        grads[at, mid : 2 * F, :] = joined.astype(bf16)
        send(f"sm{j}", piece(grads.at[at], first, 2 * F), piece(sm.at[j], first, 2 * F), to_x(-1))
        fill(0, j)

    def finish_rs(j):
        first, mid = ends[j]
        recv(f"sp{j}", piece(sp.at[j], first, 2 * F), to_x(-1))
        recv(f"sm{j}", piece(sm.at[j], first, 2 * F), to_x(1))
        at = slot(0, j)
        rows_j = slice(first, 2 * F)
        total = grads[at, rows_j, :].astype(f32) + sp[j, rows_j, :].astype(f32) + sm[j, rows_j, :].astype(f32)
        if j == 2:
            recv("ry3", ry.at[2], to_y(1))
            total = total + ry[2].astype(f32)
        if j == 0:
            return total
        grads[at, rows_j, :] = total.astype(bf16)
        send(f"ry{j}", piece(grads.at[at], first, 2 * F), piece(ry.at[j - 1], first, 2 * F), to_y(2 if j == 2 else 1))

    start_rs(3)
    early_rs()
    start_rs(2)
    product = nn(units_s[...].astype(bf16), d_logits)
    nred[...] = jnp.concatenate([product, tail], axis=0).reshape(nred.shape)
    sum_start("n", nred, nrx)
    join_rs(3)
    start_rs(1)
    join_rs(2)
    start_rs(0)
    finish_rs(3)
    join_rs(1)
    sum_middle("n", nred, nrx, nry)
    finish_rs(2)
    join_rs(0)
    sum_spread("n", nred, nrx, nry)
    finish_rs(1)
    n_high, n_low = split(sum_end("n", nred, nrx, nry))
    head_block = head_own[...].astype(bf16)
    gd_o[...] = nn(n_high, head_block) + nn(n_low, head_block)
    acc[:, 0:RB] = finish_rs(0)
    recv("ry2", ry.at[1], to_y(2))
    acc[:, 0:RB] += ry[1].astype(f32)
    recv("ry1", piece(ry.at[0], CUT, 2 * F), to_y(1))
    acc[CUT : 2 * F, 0:RB] += ry[0, CUT : 2 * F, :].astype(f32)
    gg_o[...] = acc[0:F, 0:RB]
    gu_o[...] = acc[F : 2 * F, 0:RB]
    wires.finish()


def hand_over(*refs):
    half = len(refs) // 2
    for taken, given in zip(refs[:half], refs[half:]):
        given[...] = taken[...]


def solution(mesh):
    Z = mesh.shape["shard"] // (H * C)
    names = wire_names(Z)

    def local(hidden, norm_gain, gate_codes, gate_scales, up_codes, up_scales, down_codes, down_scales, head, teacher, targets):
        T8, D = hidden.shape
        RB, F = gate_codes.shape
        B = head.shape[1]
        tokens = teacher.shape[0]
        KH = D // 2
        chunk = -(-F // (8 * X)) * 8
        vmem = pl.BlockSpec(memory_space=pltpu.VMEM)
        smem = pl.BlockSpec(memory_space=pltpu.SMEM)
        grad = jax.ShapeDtypeStruct((F, RB), f32)
        V = pltpu.VMEM
        scratch = [
            V((2, T8, KH), f32),
            V((2, T8, KH), f32),
            V((2, Z * H, 2 * T8, KH), bf16),
            V((X * Y, 2 * F, RB), bf16),
            V((128, 256), f32),
            V((LANES, RB), f32),
            V((T8, LANES), f32),
            V((LANES, tokens), f32),
            V((tokens // T8, T8, LANES), f32),
            V((2 * F, tokens), f32),
            V((F, tokens), f32),
            V((X, chunk, LANES), f32),
            V((X, chunk, LANES), f32),
            V((X, chunk, LANES), f32),
            V((X + Y, chunk, LANES), f32),
            V((X, chunk, LANES), f32),
            V((X, chunk, LANES), f32),
            V((X + Y, chunk, LANES), f32),
            V((C, Z, H, T8, LANES), f32),
            V((Z, H, T8, LANES), f32),
            V((Z, H * T8, LANES), bf16),
            V((Z, H * T8, LANES), bf16),
            V((H, T8, LANES), f32),
            V((H, T8, LANES), f32),
            V((C, Z, H * T8, LANES), bf16),
            V((H, T8, LANES), f32),
            V((X * Y, 2 * F, RB), bf16),
            V((Y, CUT, RB), bf16),
            V((Y, 2 * F - CUT, RB), bf16),
            V((Y, 2 * F, RB), bf16),
            V((Y, 2 * F, RB), bf16),
            V((Y - 1, 2 * F, RB), bf16),
            V((X, CUT, RB), bf16),
            pltpu.SemaphoreType.DMA((len(names),)),
            pltpu.SemaphoreType.DMA((len(names),)),
        ]
        loss, gate, up, down = pl.pallas_call(
            functools.partial(kernel, names, Z, D, F, B),
            out_shape=(jax.ShapeDtypeStruct((1, T8), f32), grad, grad, grad),
            in_specs=[pl.BlockSpec()] * 10 + [smem],
            out_specs=(vmem,) * 4,
            scratch_shapes=scratch,
            compiler_params=pltpu.CompilerParams(
                collective_id=0, has_side_effects=True, vmem_limit_bytes=62 << 20
            ),
            name="step",
        )(
            hidden, norm_gain.reshape(1, D), gate_codes.T, gate_scales, up_codes.T, up_scales,
            down_codes.T, down_scales, head.T, teacher.T, targets,
        )
        results = (loss, gate, up, down)
        loss, gate, up, down = pl.pallas_call(
            hand_over,
            out_shape=tuple(jax.ShapeDtypeStruct(r.shape, r.dtype) for r in results),
            in_specs=[pl.BlockSpec()] * 4,
            out_specs=(pl.BlockSpec(),) * 4,
            compiler_params=pltpu.CompilerParams(vmem_limit_bytes=62 << 20),
            name="hand_over",
        )(*results)
        return (loss.reshape(T8), gate.T, up.T, down.T)

    in_specs = (
        P(("grp", "shard"), None),
        P(),
        P("grp", "shard"),
        P("grp", "shard"),
        P("grp", "shard"),
        P("grp", "shard"),
        P("grp", "shard"),
        P("grp", "shard"),
        P(),
        P("grp", None),
        P("grp"),
    )
    out_specs = (P(("grp", "shard")), P("grp", "shard"), P("grp", "shard"), P("grp", "shard"))
    return jax.shard_map(local, mesh=mesh, in_specs=in_specs, out_specs=out_specs, check_vma=False)
```
